256 devices in a mesh: graph: 64 (over x, z, core), feat: 4 (over y).
Axes of the slice: x: 4, y: 4, z: 8, core: 2. Of those that a mesh axis runs over, the one named last changes fastest.
Arguments:
- node_lat: bfloat16 [32768, 512], P(('graph', 'feat')), may hold values from -6 to 6
- coarse_lat: bfloat16 [256, 512], replicated, may hold values from -6 to 6
- edge_lat: bfloat16 [131072, 512], P(('graph', 'feat')), may hold values from -6 to 6
- senders: int32 [131072], P(('graph', 'feat')), may hold values from 0 to 1279, as said below
- receivers: int32 [131072], P(('graph', 'feat')), may hold values from 0 to 383, as said below
- halo_rows: int32 [16384, 8], P(('graph', 'feat')), may hold values from 0 to 511, as said below
- edge_live: int32 [256], P(('graph', 'feat')), may hold values from 128 to 512, as said below
- edge_first: bfloat16 [1536, 512], P('feat'), may hold values from -0.15625 to 0.15625
- edge_second: bfloat16 [512, 512], P('feat'), may hold values from -0.25 to 0.25
- node_first: bfloat16 [1024, 512], P('feat'), may hold values from -0.1875 to 0.1875
- node_second: bfloat16 [512, 512], P('feat'), may hold values from -0.25 to 0.25
- edge_gain: float32 [512], replicated, may hold values from 0.25 to 1.75
- node_gain: float32 [512], replicated, may hold values from 0.25 to 1.75
- node_cotangent: bfloat16 [32768, 512], P(('graph', 'feat')), may hold values from -6 to 6
- coarse_cotangent: bfloat16 [256, 512], replicated, may hold values from -6 to 6
- edge_cotangent: bfloat16 [131072, 512], P(('graph', 'feat')), may hold values from -6 to 6
Outputs:
- node_grad: float32 [32768, 512], P(('graph', 'feat'))
- coarse_grad: float32 [256, 512], replicated
- edge_grad: float32 [131072, 512], P(('graph', 'feat'))
- edge_first_grad: float32 [1536, 512], P('feat')
- edge_second_grad: float32 [512, 512], P('feat')
- node_first_grad: float32 [1024, 512], P('feat')
- node_second_grad: float32 [512, 512], P('feat')
The draws below stay inside these ranges and needn't reach their ends.
Inputs may be any that keep to these rules, and one draw needn't show every extreme that they name: `senders`: codes as in the first step. `receivers`: codes as in the first step. `halo_rows`: rows within a part of 512 nodes. `edge_live`: some block is wholly live.
All inputs are finite; a program needn't handle non-finite values.
Results may differ from the reference program's by a relative error of at most 0.015.
Values may be sent and summed in bfloat16 or wider, within the bound.
A program may use at most 128 MiB of HBM per device.

```python
import jax
import jax.numpy as jnp
from jax import lax

D = 512
NODE_DEV = 128
EDGE_DEV = 512
HALO = 8
COARSE = 256
NODES = 32768
EDGES = 131072
N_GRAPH = 64
N_FEAT = 4
DEVICES = 256


def coarse_codes(key):
    return jax.random.randint(key, (EDGES,), 0, COARSE)


def draw_senders(key, part):
    key = jax.random.fold_in(key, 11)
    kind_key, inside_key, slot_key, coarse_key = jax.random.split(key, 4)
    part_rows = N_FEAT * NODE_DEV
    slot_rows = N_GRAPH * HALO
    kind_draw = jax.random.randint(kind_key, (EDGES,), 0, 20)
    inside = jax.random.randint(inside_key, (EDGES,), 0, part_rows)
    slot_draw = jax.random.randint(slot_key, (EDGES,), 0, slot_rows)
    anywhere = coarse_codes(coarse_key)
    values = jnp.where(kind_draw < 5, inside, jnp.where(kind_draw < 18, part_rows + slot_draw, part_rows + slot_rows + anywhere))
    values = values.at[0].set(0).at[EDGES - 1].set(part_rows + slot_rows + COARSE - 1)
    return values.astype(jnp.int32)


def draw_receivers(key, part):
    key = jax.random.fold_in(key, 23)
    kind_key, local_key, coarse_key = jax.random.split(key, 3)
    kind_draw = jax.random.randint(kind_key, (EDGES,), 0, 8)
    local_node = jax.random.randint(local_key, (EDGES,), 0, NODE_DEV)
    anywhere = coarse_codes(coarse_key)
    values = jnp.where(kind_draw < 7, local_node, NODE_DEV + anywhere)
    values = values.at[0].set(0).at[EDGES - 1].set(NODE_DEV + COARSE - 1)
    return values.astype(jnp.int32)


def draw_halo_rows(key, part):
    key = jax.random.fold_in(key, 37)
    part_rows = N_FEAT * NODE_DEV
    values = jax.random.randint(key, (N_GRAPH * N_FEAT * N_GRAPH, HALO), 0, part_rows)
    values = values.at[0, 0].set(0).at[-1, -1].set(part_rows - 1)
    return values.astype(jnp.int32)


def draw_edge_live(key, part):
    key = jax.random.fold_in(key, 41)
    count_key, first_key, second_key = jax.random.split(key, 3)
    blocks = N_GRAPH * N_FEAT
    values = jax.random.randint(count_key, (blocks,), EDGE_DEV // 4, EDGE_DEV + 1)
    fullest = jax.random.randint(first_key, (), 0, blocks)
    emptiest = (fullest + 1 + jax.random.randint(second_key, (), 0, blocks - 1)) % blocks
    values = values.at[fullest].set(EDGE_DEV).at[emptiest].set(EDGE_DEV // 4)
    return values.astype(jnp.int32)


def levels(stream_key, shape, pieces, smallest, high):
    factor_of = 1.0
    for dim, blocks in pieces:
        heights = jax.random.uniform(jax.random.fold_in(jax.random.fold_in(stream_key, 6), dim), (blocks,), jnp.float32, smallest / len(pieces), high / len(pieces))
        factor_of = factor_of * jnp.repeat(jnp.exp(heights), shape[dim] // blocks).reshape((-1,) + (1,) * (len(shape) - 1 - dim))
    return factor_of


def normal_values(own_key, shape, scale, reach, pieces=(), kind=jnp.bfloat16):
    factor_of = levels(own_key, shape, pieces, -0.22, 0.18) if pieces else 1.0
    drawn = jax.random.normal(own_key, shape, jnp.float32) * scale * factor_of
    return jnp.minimum(jnp.maximum(drawn, -reach), reach).astype(kind)


def setup_inputs(seed: int = 0) -> dict:
    key_list = jax.random.split(jax.random.key(seed), 17)
    node_lat = normal_values(key_list[0], (NODES, D), 1.0, 6.0, ((0, 256),))
    coarse_lat = normal_values(key_list[1], (COARSE, D), 1.0, 6.0)
    edge_lat = normal_values(key_list[2], (EDGES, D), 1.0, 6.0, ((0, 256),))
    senders = draw_senders(jax.random.fold_in(key_list[16], 71), 0)
    receivers = draw_receivers(jax.random.fold_in(key_list[16], 71), 0)
    halo_rows = draw_halo_rows(jax.random.fold_in(key_list[16], 71), 0)
    edge_live = draw_edge_live(jax.random.fold_in(key_list[16], 71), 0)
    edge_first = normal_values(key_list[7], (3 * D, D), (3 * D) ** -0.5, 0.15625, ((0, 4),))
    edge_second = normal_values(key_list[8], (D, D), D ** -0.5, 0.25, ((0, 4),))
    node_first = normal_values(key_list[9], (2 * D, D), (2 * D) ** -0.5, 0.1875, ((0, 4),))
    node_second = normal_values(key_list[10], (D, D), D ** -0.5, 0.25, ((0, 4),))
    edge_gain = jnp.clip(1.0 + 0.15 * jax.random.normal(key_list[11], (D,), jnp.float32), 0.25, 1.75)
    node_gain = jnp.clip(1.0 + 0.15 * jax.random.normal(key_list[12], (D,), jnp.float32), 0.25, 1.75)
    node_cotangent = normal_values(key_list[13], (NODES, D), 1.0, 6.0, ((0, 256),))
    coarse_cotangent = normal_values(key_list[14], (COARSE, D), 1.0, 6.0)
    edge_cotangent = normal_values(key_list[15], (EDGES, D), 1.0, 6.0, ((0, 256),))
    return {"node_lat": node_lat, "coarse_lat": coarse_lat, "edge_lat": edge_lat, "senders": senders, "receivers": receivers, "halo_rows": halo_rows, "edge_live": edge_live, "edge_first": edge_first, "edge_second": edge_second, "node_first": node_first, "node_second": node_second, "edge_gain": edge_gain, "node_gain": node_gain, "node_cotangent": node_cotangent, "coarse_cotangent": coarse_cotangent, "edge_cotangent": edge_cotangent}


NORM_EPSILON = 1e-05

def contract_rows(left, right):
    return lax.dot_general(left, right, (((0,), (0,)), ((), ())), preferred_element_type=jnp.float32)

def contract_last(left, right):
    return lax.dot_general(left, right, (((1,), (1,)), ((), ())), preferred_element_type=jnp.float32)

def mlp_forward(inputs, first, second):
    before = jnp.dot(inputs, first, preferred_element_type=jnp.float32)
    hidden = (before * jax.nn.sigmoid(before)).astype(jnp.bfloat16)
    output = jnp.dot(hidden, second, preferred_element_type=jnp.float32)
    centred = output - lax.optimization_barrier(jnp.mean(output, axis=1, keepdims=True))
    inverse = lax.rsqrt(lax.optimization_barrier(jnp.mean(centred * centred, axis=1, keepdims=True)) + NORM_EPSILON)
    return (before, hidden, centred * inverse, inverse)

def mlp_backward(inputs, first, second, gain, saved, upstream):
    before, hidden, normed, inverse = saved
    scaled = upstream * gain
    grad_lin = inverse * (scaled - lax.optimization_barrier(jnp.mean(scaled, axis=1, keepdims=True)) - normed * lax.optimization_barrier(jnp.mean(scaled * normed, axis=1, keepdims=True)))
    grad_lin = grad_lin.astype(jnp.bfloat16)
    grad_hidden = contract_last(grad_lin, second)
    sigma = jax.nn.sigmoid(before)
    grad_before = (grad_hidden * sigma * (1.0 + before * (1.0 - sigma))).astype(jnp.bfloat16)
    grad_inputs = contract_last(grad_before, first)
    grad_second = contract_rows(hidden, grad_lin)
    grad_first = contract_rows(inputs, grad_before)
    return (grad_inputs, grad_first, grad_second)

def reference(node_lat, coarse_lat, edge_lat, senders, receivers, halo_rows, edge_live, edge_first, edge_second, node_first, node_second, edge_gain, node_gain, node_cotangent, coarse_cotangent, edge_cotangent):
    part_rows = N_FEAT * NODE_DEV
    slot_rows = N_GRAPH * HALO
    table_rows = NODES + COARSE
    device_of = jnp.arange(EDGES, dtype=jnp.int32) // EDGE_DEV
    graph_of = device_of // N_FEAT
    feat_of = device_of % N_FEAT
    offset = jnp.clip(senders - part_rows, 0, slot_rows - 1).astype(jnp.int32)
    source_graph = offset // HALO
    flat_halo = halo_rows.reshape(-1)
    halo_index = (((source_graph * N_FEAT + feat_of) * N_GRAPH + graph_of) * HALO + offset % HALO).astype(jnp.int32)
    remote = source_graph * part_rows + flat_halo[halo_index]
    local_part = graph_of * part_rows + jnp.clip(senders, 0, part_rows - 1)
    coarse_send = NODES + jnp.clip(senders - part_rows - slot_rows, 0, COARSE - 1)
    send_global = jnp.where(senders < part_rows, local_part, jnp.where(senders < part_rows + slot_rows, remote, coarse_send)).astype(jnp.int32)
    recv_global = jnp.where(receivers < NODE_DEV, device_of * NODE_DEV + receivers, NODES + receivers - NODE_DEV).astype(jnp.int32)
    position = jnp.arange(EDGES, dtype=jnp.int32) % EDGE_DEV
    alive_mask = (position < edge_live[device_of]).astype(jnp.float32)[:, None]
    node_table = jnp.concatenate([node_lat, coarse_lat], axis=0)
    blocks = (edge_lat.reshape(DEVICES, EDGE_DEV, D), send_global.reshape(DEVICES, EDGE_DEV), recv_global.reshape(DEVICES, EDGE_DEV), alive_mask.reshape(DEVICES, EDGE_DEV, 1), edge_cotangent.reshape(DEVICES, EDGE_DEV, D))

    def edge_inputs(edge_rows, send_block, recv_block):
        return jnp.concatenate([edge_rows, node_table[send_block], node_table[recv_block]], axis=1)

    def forward_block(block):
        edge_rows, send_block, recv_block, mask_block, unused = block
        saved = mlp_forward(edge_inputs(edge_rows, send_block, recv_block), edge_first, edge_second)
        return (edge_rows.astype(jnp.float32) + mask_block * (saved[2] * edge_gain)).astype(jnp.bfloat16)
    edge_next = lax.map(forward_block, blocks).reshape(EDGES, D)
    aggregate = jax.ops.segment_sum(alive_mask * edge_next.astype(jnp.float32), recv_global, num_segments=table_rows)
    node_inputs = jnp.concatenate([node_table, aggregate.astype(jnp.bfloat16)], axis=1)
    node_saved = mlp_forward(node_inputs, node_first, node_second)
    node_upstream = jnp.concatenate([node_cotangent, coarse_cotangent], axis=0).astype(jnp.float32)
    grad_nodes, node_first_grad, node_second_grad = mlp_backward(node_inputs, node_first, node_second, node_gain, node_saved, node_upstream)
    grad_start = node_upstream + grad_nodes[:, :D]
    grad_aggregate = grad_nodes[:, D:]

    def backward_block(carry, block):
        grad_table, first_sum, second_sum = carry
        edge_rows, send_block, recv_block, mask_block, cot_block = block
        inputs = edge_inputs(edge_rows, send_block, recv_block)
        saved_block = mlp_forward(inputs, edge_first, edge_second)
        grad_next = cot_block.astype(jnp.float32) + mask_block * grad_aggregate[recv_block]
        grad_inputs, grad_first, grad_second = mlp_backward(inputs, edge_first, edge_second, edge_gain, saved_block, mask_block * grad_next)
        grad_table = grad_table.at[send_block].add(grad_inputs[:, D:2 * D])
        grad_table = grad_table.at[recv_block].add(grad_inputs[:, 2 * D:])
        return ((grad_table, first_sum + grad_first, second_sum + grad_second), grad_next + grad_inputs[:, :D])
    start_carry = (grad_start, jnp.zeros((3 * D, D), jnp.float32), jnp.zeros((D, D), jnp.float32))
    (grad_table, edge_first_grad, edge_second_grad), edge_grad = lax.scan(backward_block, start_carry, blocks)
    return (grad_table[:NODES], grad_table[NODES:], edge_grad.reshape(EDGES, D), edge_first_grad, edge_second_grad, node_first_grad, node_second_grad)
```

```python
import functools

import jax
import jax.numpy as jnp
from jax import lax
from jax.experimental import pallas as pl
from jax.experimental.pallas import tpu as pltpu
from jax.sharding import PartitionSpec as P

NORM_EPSILON = 1e-05
F32 = jnp.float32
BF16 = jnp.bfloat16
MESH = pl.DeviceIdType.MESH

D = 512
N = 128
E = 512
C = 256
NX, NY, NZ, NC = 4, 4, 8, 2
G = NX * NZ * NC
HALO = 8
RE, RN = 256, 192
ZR = 32
PLANE = NX * NZ


def dot(a, b):
    return jnp.dot(a, b, preferred_element_type=F32)


def dot_nt(a, b):
    return lax.dot_general(a, b, (((1,), (1,)), ((), ())), preferred_element_type=F32)


def dot_tn(a, b):
    return lax.dot_general(a, b, (((0,), (0,)), ((), ())), preferred_element_type=F32)


def xor4(v, j):
    return (v, v + 1 - 2 * (v % 2), (v + 2) % 4, 3 - v)[j]


def aligned(index, by):
    return pl.multiple_of(index, by)


def normalise(output):
    centred = output - jnp.mean(output, axis=1, keepdims=True)
    inverse = lax.rsqrt(jnp.mean(centred * centred, axis=1, keepdims=True) + NORM_EPSILON)
    return centred * inverse, inverse


def norm_backward(upstream, gain, normed, inverse):
    scaled = upstream * gain
    grad = inverse * (
        scaled
        - jnp.mean(scaled, axis=1, keepdims=True)
        - normed * jnp.mean(scaled * normed, axis=1, keepdims=True)
    )
    return grad.astype(BF16)


def silu_backward(grad_hidden, before):
    sigma = jax.nn.sigmoid(before)
    return (grad_hidden * sigma * (1.0 + before * (1.0 - sigma))).astype(BF16)


SCRATCH = dict(
    nodes=((NY, N, D), BF16),
    ef=((3 * D, D), BF16),
    es=((D, D), BF16),
    nf=((2 * D, D), BF16),
    ns=((D, D), BF16),
    halo_hot=((G * HALO, NY * N), BF16),
    halo_hot_t=((NY * N, G * HALO), BF16),
    send_hot=((E, 1280), BF16),
    send_hot_t=((1280, E), BF16),
    recv_hot=((E, N + C), BF16),
    recv_hot_t=((N + C, E), BF16),
    out_slots=((G, 16, 256), BF16),
    in_slots=((G, 16, 256), BF16),
    back_out=((G, 16, 256), BF16),
    back_in=((G, 16, 256), BF16),
    halo=((G * HALO, D), BF16),
    edge_in=((E, 3 * D), BF16),
    before=((E, D), F32),
    hidden=((E, D), BF16),
    normed=((E, D), F32),
    inverse=((E, 1), F32),
    lin=((E, D), BF16),
    gbefore=((E, D), BF16),
    gnext=((E, D), F32),
    moved=((E, D), BF16),
    node_in=((N + C, 2 * D), BF16),
    n_before=((N + C, D), F32),
    n_hidden=((N + C, D), BF16),
    n_normed=((N + C, D), F32),
    n_inverse=((N + C, 1), F32),
    n_lin=((N + C, D), BF16),
    n_gbefore=((N + C, D), BF16),
    direct=((N + C, D), F32),
    gagg=((N + C, D), BF16),
    coarse_total=((C, D), BF16),
    coarse_part=((C, D), F32),
    recv_own=((N, D), F32),
    part_grads=((NY * N, D), F32),
    a1_src=((32, 16, 256), BF16),
    a1_rs=((32, 16, 256), BF16),
    a1_z=((NZ, 16, 256), BF16),
    a1_ag=((32, 16, 256), BF16),
    a2_src=((32, 16, 256), BF16),
    a2_rs=((32, 16, 256), BF16),
    a2_z=((NZ, 16, 256), BF16),
    a2_ag=((32, 16, 256), BF16),
    v_node_cot=((N, D), BF16),
    v_coarse_cot=((C, D), BF16),
    v_edge_cot=((E, D), BF16),
    v_edge_grad=((E, D), F32),
    v_node_grad=((N, D), F32),
    v_coarse_grad=((C, D), F32),
    p_y=((NY, N, D), BF16),
    p_a1=((2, N // 2, D), BF16),
    p_b1=((2, N // 2, D), BF16),
    p_a2=((N // 2, D), BF16),
    p_b2=((N // 2, D), BF16),
)


def job_scratch(r):
    return dict(
        w=((NY, 2 * r, D), BF16),
        c=((NY, r, D), BF16),
        y=((NY, r, D), BF16),
        ya1=((2, r // 2, D), BF16),
        yb1=((2, r // 2, D), BF16),
        ya2=((r // 2, D), BF16),
        yb2=((r // 2, D), BF16),
        sum=((r, D), F32),
    )


EDGE_JOB, NODE_JOB = job_scratch(RE), job_scratch(RN)
EDGE_JOB.update(
    ps=((PLANE, 16, 256), BF16),
    pr=((PLANE, 16, 256), BF16),
    g=((PLANE, 16, 256), BF16),
)
NODE_JOB.update(
    x=((NX, RN, 128), BF16),
    xa1=((2, RN // 2, 128), BF16),
    xb1=((2, RN // 2, 128), BF16),
    xa2=((RN // 2, 128), BF16),
    xb2=((RN // 2, 128), BF16),
    zs=((NZ, ZR, 128), BF16),
    zr=((NZ, ZR, 128), BF16),
    g=((NX, NZ, ZR, 128), BF16),
    extra=((NC, NZ * ZR, D), F32),
)
SENDS, LOCALS = 76, 16

SMALL, LARGE = True, False
INPUTS = dict(
    node_lat=LARGE, coarse_lat=LARGE, edge_lat=LARGE, senders=SMALL, receivers=SMALL, halo_rows=SMALL,
    edge_live=SMALL, w_ef=LARGE, w_es=LARGE, w_nf=LARGE, w_ns=LARGE, edge_gain=SMALL, node_gain=SMALL,
    node_cot=LARGE, coarse_cot=LARGE, edge_cot=LARGE,
)
OUTPUTS = dict(
    node_grad=((N, D), F32),
    coarse_grad=((C, D), F32),
    edge_grad=((E, D), F32),
    e_grad=((NC, PLANE, 16, 256), BF16),
    n_grad=((NC, NX, NZ, ZR, 128), BF16),
)


class Refs(dict):
    __getattr__ = dict.__getitem__


class Links:
    def __init__(self, send_sems, recv_sems, local_sems):
        self.send_sems, self.recv_sems, self.used, self.sent = send_sems, recv_sems, 0, []
        self.local_sems, self.local_used = local_sems, 0
        graph = lax.axis_index("graph")
        self.g, self.y = graph, lax.axis_index("feat")
        self.c, self.z, self.x = graph % 2, (graph // 2) % 8, graph // 16

    def slot(self):
        self.used += 1
        return self.used - 1

    def at(self, x=None, y=None, z=None, c=None):
        x = self.x if x is None else x
        y = self.y if y is None else y
        z = self.z if z is None else z
        c = self.c if c is None else c
        return ((x * 8 + z) * 2 + c, y)

    def local(self, src, dst):
        copy = pltpu.make_async_copy(src, dst, self.local_sems.at[self.local_used])
        self.local_used += 1
        copy.start()
        return copy

    def send(self, src, dst, device):
        k = self.slot()
        copy = pltpu.make_async_remote_copy(
            src_ref=src,
            dst_ref=dst,
            send_sem=self.send_sems.at[k],
            recv_sem=self.recv_sems.at[k],
            device_id=device,
            device_id_type=MESH,
        )
        copy.start()
        self.sent.append(copy)
        return copy

    def send_many(self, count, peer, src, dst, whole):
        k = self.slot()

        def body(j, carry):
            index, device = peer(j)
            pltpu.make_async_remote_copy(
                src_ref=src(index),
                dst_ref=dst,
                send_sem=self.send_sems.at[k],
                recv_sem=self.recv_sems.at[k],
                device_id=device,
                device_id_type=MESH,
            ).start()
            return carry

        lax.fori_loop(1, count, body, 0)
        self.sent.append(("many", whole, k))

        def wait():
            pltpu.make_async_copy(whole, whole, self.recv_sems.at[k]).wait()

        return wait

    def finish(self):
        for copy in self.sent:
            if isinstance(copy, tuple):
                pltpu.make_async_copy(copy[1], copy[1], self.send_sems.at[copy[2]]).wait()
            else:
                copy.wait_send()


def to_slots(rows):
    rows = rows.reshape(G, HALO, D)
    return jnp.concatenate([rows[:, :, :256], rows[:, :, 256:]], axis=1).astype(BF16)


def from_slots(slots):
    slots = slots.astype(F32)
    rows = jnp.concatenate([slots[:, :8, :], slots[:, 8:, :]], axis=2)
    return rows.reshape(G * HALO, D).astype(BF16)


def halving(links, buf, half, ra1, rb1, ra2, rb2, partner, total_out):
    lo, hi = pl.ds(0, half), pl.ds(half, half)
    p1, p3 = partner(1), partner(3)
    a = links.send(buf.at[pl.ds(1, 2), lo], ra1, p1)
    b = links.send(buf.at[pl.ds(2, 2), hi], rb1, p3)
    yield
    a.wait_recv()
    buf[3, lo] = (buf[3, lo].astype(F32) + ra1[1].astype(F32)).astype(BF16)
    a = links.send(buf.at[3, lo], ra2, p3)
    b.wait_recv()
    buf[1, hi] = (buf[1, hi].astype(F32) + rb1[0].astype(F32)).astype(BF16)
    b = links.send(buf.at[1, hi], rb2, p1)
    total_out[lo] = buf[0, lo].astype(F32) + ra1[0].astype(F32)
    total_out[hi] = buf[0, hi].astype(F32) + rb1[1].astype(F32)
    yield
    a.wait_recv()
    total_out[lo] = total_out[lo] + ra2[...].astype(F32)
    b.wait_recv()
    total_out[hi] = total_out[hi] + rb2[...].astype(F32)


def coarse_sum(links, source, src, rs, zb, ag, out):
    me = (links.x * 4 + links.y) * 2 + links.c

    def peer(j):
        m = (me + j * 11) % 32
        return m, links.at(x=m // 8, y=(m // 2) % 4, c=m % 2)

    for i in range(32):
        src[i] = source[(i // 2) * 16 : (i // 2) * 16 + 16, (i % 2) * 256 : (i % 2) * 256 + 256].astype(BF16)
    wait = links.send_many(32, peer, lambda m: src.at[m], rs.at[me], rs.at[pl.ds(0, 31)])
    rs[me] = src[me]
    yield
    wait()
    zb[links.z] = jnp.sum(rs[...].astype(F32), axis=0).astype(BF16)

    def along(j):
        to = (links.z + j * 3) % 8
        return to, links.at(z=to)

    wait = links.send_many(8, along, lambda m: zb.at[links.z], zb.at[links.z], zb.at[pl.ds(0, 7)])
    yield
    wait()
    ag[me] = jnp.sum(zb[...].astype(F32), axis=0).astype(BF16)
    wait = links.send_many(32, peer, lambda m: ag.at[me], ag.at[me], ag.at[pl.ds(0, 31)])
    yield
    wait()
    for i in range(32):
        out[(i // 2) * 16 : (i // 2) * 16 + 16, (i % 2) * 256 : (i % 2) * 256 + 256] = ag[i].astype(out.dtype)


def weight_scatter(links, t, r, fill):
    w, cin, ybuf = t.w, t.c, t.y
    other = links.at(c=1 - links.c)
    theirs = pl.ds(aligned((1 - links.c) * r, 16), r)
    mine = pl.ds(aligned(links.c * r, 16), r)
    copies = {}
    for j in (2, 1, 3, 0):
        fill(j, xor4(links.y, j))
        copies[j] = links.send(w.at[j, theirs], cin.at[j], other)
    yield
    for j in (2, 1, 3, 0):
        copies[j].wait_recv()
        ybuf[j] = (w[j, mine].astype(F32) + cin[j].astype(F32)).astype(BF16)
    total = t.sum
    yield from halving(
        links, ybuf, r // 2, t.ya1, t.yb1, t.ya2, t.yb2,
        lambda j: links.at(y=xor4(links.y, j)), total,
    )


def edge_weights_sum(links, t, r, fill, out):
    yield from weight_scatter(links, t, r, fill)
    total, ps, pr, gathered = t.sum, t.ps, t.pr, t.g
    for i in range(PLANE):
        ps[i] = total[(i // 2) * 16 : (i // 2) * 16 + 16, (i % 2) * 256 : (i % 2) * 256 + 256].astype(BF16)
    me = links.x * NZ + links.z

    def peer(k):
        m = (me + k * 11) % PLANE
        return m, links.at(x=m // NZ, z=m % NZ)

    wait = links.send_many(PLANE, peer, lambda m: ps.at[m], pr.at[me], pr.at[pl.ds(0, PLANE - 1)])
    pr[me] = ps[me]
    yield
    wait()
    gathered[me] = jnp.sum(pr[...].astype(F32), axis=0).astype(BF16)
    wait = links.send_many(
        PLANE, peer, lambda m: gathered.at[me], gathered.at[me], gathered.at[pl.ds(0, PLANE - 1)]
    )
    yield
    wait()
    copy = links.send(gathered, out.at[links.c], links.at(c=1 - links.c))
    own = links.local(gathered, out.at[links.c])
    yield
    copy.wait_recv()
    own.wait()


def node_weights_sum(links, t, r, fill, out):
    yield from weight_scatter(links, t, r, fill)
    for j in range(4):
        t.x[j] = t.sum[:, pl.ds(aligned(xor4(links.x, j) * 128, 128), 128)].astype(BF16)
    sub = t.sum.at[:, pl.ds(0, 128)]
    yield from halving(
        links, t.x, r // 2, t.xa1, t.xb1, t.xa2, t.xb2, lambda j: links.at(x=xor4(links.x, j)), sub
    )
    blocks = r // ZR
    for i in range(NZ):
        t.zs[i] = sub[i * ZR : (i + 1) * ZR].astype(BF16) if i < blocks else jnp.zeros((ZR, 128), BF16)

    def along(j):
        to = (links.z + j * 3) % NZ
        return to, links.at(z=to)

    wait = links.send_many(NZ, along, lambda m: t.zs.at[m], t.zr.at[links.z], t.zr.at[pl.ds(0, NZ - 1)])
    t.zr[links.z] = t.zs[links.z]
    yield
    wait()
    own = t.g.at[links.x]
    extra = t.extra[
        links.c, pl.ds(aligned(links.z * ZR, ZR), ZR), pl.ds(aligned(links.x * 128, 128), 128)
    ]
    own[links.z] = (jnp.sum(t.zr[...].astype(F32), axis=0) + extra).astype(BF16)
    wait = links.send_many(NZ, along, lambda m: own.at[links.z], own.at[links.z], own.at[pl.ds(0, NZ - 1)])
    yield
    wait()
    x1, x2, x3 = xor4(links.x, 1), xor4(links.x, 2), xor4(links.x, 3)
    every, lo, hi = pl.ds(0, blocks), pl.ds(0, blocks // 2), pl.ds(blocks // 2, blocks // 2)
    mine = t.g.at[links.x, every]
    a = links.send(mine, mine, links.at(x=x1))
    b = links.send(mine, mine, links.at(x=x3))
    yield
    a.wait_recv()
    a = links.send(t.g.at[x1, lo], t.g.at[x1, lo], links.at(x=x3))
    b.wait_recv()
    b = links.send(t.g.at[x3, hi], t.g.at[x3, hi], links.at(x=x1))
    yield
    a.wait_recv()
    b.wait_recv()
    result = t.g.at[:, every]
    copy = links.send(result, out.at[links.c, :, every], links.at(c=1 - links.c))
    local = links.local(result, out.at[links.c, :, every])
    yield
    copy.wait_recv()
    local.wait()


def body(*refs):
    refs = iter(refs)
    s = Refs(zip([*INPUTS, *OUTPUTS, *SCRATCH], refs))
    edge_refs, node_refs = Refs(zip(EDGE_JOB, refs)), Refs(zip(NODE_JOB, refs))
    links = Links(*refs)
    x, y, z, c, g = links.x, links.y, links.z, links.c, links.g
    y1, y2, y3 = xor4(y, 1), xor4(y, 2), xor4(y, 3)
    other = links.at(c=1 - c)
    ef, es, nf, ns = s.ef, s.es, s.nf, s.ns
    weights = {"ef": 384, "es": 128, "nf": 256, "ns": 128}
    nodes, edge_in, node_in = s.nodes, s.edge_in, s.node_in

    barrier = pltpu.get_barrier_semaphore()

    def greet_graph(j, carry):
        pl.semaphore_signal(barrier, inc=1, device_id=((g + j) % G, y), device_id_type=MESH)
        return carry

    def greet_plane(j, carry):
        k = j // 3
        device = links.at(x=k // 2, c=k % 2, y=(y + 1 + j % 3) % 4)
        pl.semaphore_signal(barrier, inc=1, device_id=device, device_id_type=MESH)
        return carry

    lax.fori_loop(1, G, greet_graph, 0)
    lax.fori_loop(0, 24, greet_plane, 0)
    early = [
        links.local(s.node_lat, nodes.at[y]),
        links.local(s.node_lat, node_in.at[pl.ds(0, N), pl.ds(0, D)]),
        links.local(s.coarse_lat, node_in.at[pl.ds(N, C), pl.ds(0, D)]),
        links.local(s.edge_lat, edge_in.at[:, pl.ds(0, D)]),
    ]
    for name, rows in weights.items():
        early.append(links.local(s["w_" + name], s[name].at[pl.ds(aligned(y * rows, 16), rows)]))
    for name in ("node_cot", "coarse_cot", "edge_cot"):
        early.append(links.local(s[name], s["v_" + name]))
    pl.semaphore_wait(barrier, G - 1 + 24)

    lo, hi = pl.ds(0, N // 2), pl.ds(N // 2, N // 2)
    lat = s.node_lat
    a_lo = links.send(lat.at[lo], nodes.at[y, lo], links.at(y=y1))
    b_hi = links.send(lat.at[hi], nodes.at[y, hi], links.at(y=y3))
    a_hi = links.send(lat.at[hi], nodes.at[y, hi], links.at(y=y1))
    b_lo = links.send(lat.at[lo], nodes.at[y, lo], links.at(y=y3))

    lanes = lax.broadcasted_iota(jnp.int32, (E, 128), 1)
    subs = lax.broadcasted_iota(jnp.int32, (128, E), 0)

    def hot(code_row, hot_ref, hot_t_ref, width):
        across = jnp.broadcast_to(code_row, (128, E))
        down = jnp.transpose(across)
        for j in range(width // 128):
            hot_ref[:, j * 128 : (j + 1) * 128] = jnp.where(down == lanes + j * 128, 1.0, 0.0).astype(BF16)
            hot_t_ref[j * 128 : (j + 1) * 128, :] = jnp.where(across == subs + j * 128, 1.0, 0.0).astype(BF16)

    codes = s.halo_rows[...]
    spread = (
        lax.broadcasted_iota(jnp.int32, (G, G * HALO), 0)
        == lax.broadcasted_iota(jnp.int32, (G, G * HALO), 1) // HALO
    )
    spread = jnp.where(spread, 1.0, 0.0).astype(BF16)
    high = dot((codes // 16).astype(F32).astype(BF16), spread)
    low = dot((codes % 16).astype(F32).astype(BF16), spread)
    shape = (HALO, G * HALO)
    at_k = lax.broadcasted_iota(jnp.int32, shape, 0) == lax.broadcasted_iota(jnp.int32, shape, 1) % HALO
    codes = jnp.sum(jnp.where(at_k, high * 16.0 + low, 0.0), axis=0, keepdims=True).astype(jnp.int32)
    hot(codes, s.halo_hot, s.halo_hot_t, NY * N)
    for copy in early:
        copy.wait()

    a_lo.wait_recv()
    a2 = links.send(nodes.at[y1, lo], nodes.at[y1, lo], links.at(y=y3))
    b_hi.wait_recv()
    b2 = links.send(nodes.at[y3, hi], nodes.at[y3, hi], links.at(y=y1))

    def weight_rows(name, owner, first, count):
        rows = weights[name]
        return s[name].at[pl.ds(aligned(owner * rows + c * (rows // 2) + first, 16), count)]

    def weight_step1(group):
        copies = []
        for name in group:
            half = weights[name] // 2
            src = s["w_" + name].at[pl.ds(aligned(c * half, 16), half)]
            copies.append(
                (
                    name,
                    links.send(src, weight_rows(name, y, 0, half), links.at(y=y1)),
                    links.send(src, weight_rows(name, y, 0, half), links.at(y=y3)),
                )
            )
        return copies

    def weight_step2(copies):
        forward, swap = [], []
        for name, first, second in copies:
            half, quarter = weights[name] // 2, weights[name] // 4
            first.wait_recv()
            src = weight_rows(name, y1, 0, quarter)
            forward.append(links.send(src, src, links.at(y=y3)))
            src = weight_rows(name, y1, 0, half)
            swap.append(links.send(src, src, other))
            second.wait_recv()
            src = weight_rows(name, y3, quarter, quarter)
            forward.append(links.send(src, src, links.at(y=y1)))
            src = weight_rows(name, y3, 0, half)
            swap.append(links.send(src, src, other))
        return forward, swap

    def weight_step3(group, forward, swap):
        for copy in forward:
            copy.wait_recv()
        for name in group:
            src = weight_rows(name, y2, 0, weights[name] // 2)
            swap.append(links.send(src, src, other))
        return swap

    for copy in (a_hi, b_lo, a2, b2):
        copy.wait_recv()
    edge_weights = weight_step1(("ef", "es"))

    out_slots, in_slots = s.out_slots, s.in_slots
    part_nodes = nodes[...].reshape(NY * N, D)
    out_slots[...] = to_slots(dot(s.halo_hot[...], part_nodes))

    def graph_peer(j):
        to = (g + j * 29) % G
        return to, (to, y)

    halo_wait = links.send_many(
        G, graph_peer, lambda m: out_slots.at[m], in_slots.at[g], in_slots.at[pl.ds(0, G - 1)]
    )
    in_slots[g] = out_slots[g]

    live = s.edge_live[...]
    alive_row = lax.broadcasted_iota(jnp.int32, (1, E), 1) < live
    hot(jnp.where(alive_row, s.senders[...], -1), s.send_hot, s.send_hot_t, 1280)
    hot(jnp.where(alive_row, s.receivers[...], -1), s.recv_hot, s.recv_hot_t, N + C)
    node_lat, coarse_lat = node_in[:N, :D], node_in[N:, :D]
    edge_in[:, 2 * D :] = (
        dot(s.recv_hot[:, :N], node_lat) + dot(s.recv_hot[:, N:], coarse_lat)
    ).astype(BF16)
    edge_in[:, D : 2 * D] = (
        dot(s.send_hot[:, :512], part_nodes) + dot(s.send_hot[:, 1024:], coarse_lat)
    ).astype(BF16)
    edge_forward, edge_swap = weight_step2(edge_weights)
    node_weights = weight_step1(("nf", "ns"))
    edge_swap = weight_step3(("ef", "es"), edge_forward, edge_swap)
    for copy in edge_swap:
        copy.wait_recv()
    before = s.before
    before[...] = dot(edge_in[:, :D], ef[:D]) + dot(edge_in[:, 2 * D :], ef[2 * D :])

    node_forward, node_swap = weight_step2(node_weights)

    halo_wait()
    s.halo[...] = from_slots(in_slots[...])
    edge_in[:, D : 2 * D] = (
        edge_in[:, D : 2 * D].astype(F32) + dot(s.send_hot[:, 512:1024], s.halo[...])
    ).astype(BF16)
    before[...] = before[...] + dot(edge_in[:, D : 2 * D], ef[D : 2 * D])
    s.hidden[...] = (before[...] * jax.nn.sigmoid(before[...])).astype(BF16)
    normed, inverse = normalise(dot(s.hidden[...], es[...]))
    s.normed[...] = normed
    s.inverse[...] = inverse
    edge_next = (edge_in[:, :D].astype(F32) + normed * s.edge_gain[...]).astype(BF16)
    s.coarse_part[...] = dot(s.recv_hot_t[N:], edge_next)
    total = coarse_sum(
        links, s.coarse_part, s.a1_src, s.a1_rs, s.a1_z, s.a1_ag, s.coarse_total
    )
    next(total)
    own_agg = dot(s.recv_hot_t[:N], edge_next).astype(BF16)
    node_in[:N, D:] = own_agg
    node_swap = weight_step3(("nf", "ns"), node_forward, node_swap)

    def node_up(rows):
        name = "v_node_cot" if rows.start == 0 else "v_coarse_cot"
        return s[name][...].astype(F32)

    def node_pass_forward(rows):
        a = dot(node_in[rows], nf[...])
        hidden = (a * jax.nn.sigmoid(a)).astype(BF16)
        s.n_before[rows] = a
        s.n_hidden[rows] = hidden
        n, inv = normalise(dot(hidden, ns[...]))
        s.n_normed[rows] = n
        s.n_inverse[rows] = inv

    def node_pass_backward(rows):
        up = node_up(rows)
        q = norm_backward(up, s.node_gain[...], s.n_normed[rows], s.n_inverse[rows])
        zz = silu_backward(dot_nt(q, ns[...]), s.n_before[rows])
        s.n_lin[rows] = q
        s.n_gbefore[rows] = zz
        s.direct[rows] = up + dot_nt(zz, nf[:D])
        s.gagg[rows] = dot_nt(zz, nf[D:]).astype(BF16)

    own, coarse = slice(0, N), slice(N, N + C)

    def fill_node(j, to):
        w = node_refs.w
        w[j, :256] = dot_tn(node_in[:N, pl.ds(aligned(to * 256, 128), 256)], s.n_gbefore[:N]).astype(BF16)
        w[j, 256:] = dot_tn(s.n_hidden[:N, pl.ds(aligned(to * 128, 128), 128)], s.n_lin[:N]).astype(BF16)

    node_job = node_weights_sum(links, node_refs, RN, fill_node, s.n_grad)
    next(total)
    for copy in node_swap:
        copy.wait_recv()
    node_pass_forward(own)
    node_pass_backward(own)
    next(node_job)
    next(total)
    next(node_job)
    for _ in total:
        pass
    node_in[N:, D:] = s.coarse_total[...]
    node_pass_forward(coarse)
    node_pass_backward(coarse)

    s.gnext[...] = s.v_edge_cot[...].astype(F32) + dot(s.recv_hot[...], s.gagg[...])
    alive = lax.broadcasted_iota(jnp.int32, (E, 1), 0) < live
    upstream = jnp.where(alive, s.gnext[...], 0.0)
    q = norm_backward(upstream, s.edge_gain[...], s.normed[...], s.inverse[...])
    s.lin[...] = q
    s.gbefore[...] = silu_backward(dot_nt(q, es[...]), before[...])
    gbefore = s.gbefore

    def fill_edge(j, to):
        w = edge_refs.w
        w[j, :384] = dot_tn(edge_in[:, pl.ds(aligned(to * 384, 128), 384)], gbefore[...]).astype(BF16)
        w[j, 384:] = dot_tn(s.hidden[:, pl.ds(aligned(to * 128, 128), 128)], s.lin[...]).astype(BF16)

    edge_job = edge_weights_sum(links, edge_refs, RE, fill_edge, s.e_grad)
    next(edge_job)
    moved = s.moved
    moved[...] = dot_nt(gbefore[...], ef[D : 2 * D]).astype(BF16)
    back_out, back_in = s.back_out, s.back_in
    back_out[...] = to_slots(dot(s.send_hot_t[512:1024], moved[...]))
    back_wait = links.send_many(
        G, graph_peer, lambda m: back_out.at[m], back_in.at[g], back_in.at[pl.ds(0, G - 1)]
    )
    back_in[g] = back_out[g]
    next(edge_job)
    next(node_job)
    s.part_grads[...] = dot(s.send_hot_t[:512], moved[...])
    s.coarse_part[...] = dot(s.send_hot_t[1024:], moved[...])
    moved[...] = dot_nt(gbefore[...], ef[2 * D :]).astype(BF16)
    s.coarse_part[...] = s.coarse_part[...] + dot(s.recv_hot_t[N:], moved[...])
    coarse_grad = s.v_coarse_grad
    total = coarse_sum(links, s.coarse_part, s.a2_src, s.a2_rs, s.a2_z, s.a2_ag, coarse_grad)
    next(total)
    next(node_job)
    s.recv_own[...] = dot(s.recv_hot_t[:N], moved[...])
    s.v_edge_grad[...] = s.gnext[...] + dot_nt(gbefore[...], ef[:D])
    edge_out = links.local(s.v_edge_grad, s.edge_grad)
    extra = node_refs.extra
    first = dot_tn(node_in[N:, pl.ds(aligned(y * 256, 128), 256)], s.n_gbefore[N:])
    extra[0, :RN] = first[:RN]
    extra[1, : 256 - RN] = first[RN:]
    extra[1, 256 - RN : RN] = dot_tn(s.n_hidden[N:, pl.ds(aligned(y * 128, 128), 128)], s.n_lin[N:])
    extra[:, RN:] = jnp.zeros((NC, NZ * ZR - RN, D), F32)
    next(edge_job)
    next(node_job)
    next(total)

    back_wait()
    s.halo[...] = from_slots(back_in[...])
    s.part_grads[...] = s.part_grads[...] + dot(s.halo_hot_t[...], s.halo[...])
    p_y = s.p_y
    for j in range(4):
        p_y[j] = s.part_grads[pl.ds(aligned(xor4(y, j) * N, 16), N), :].astype(BF16)
    node_grad = s.v_node_grad
    part_job = halving(
        links, p_y, N // 2, s.p_a1, s.p_b1, s.p_a2, s.p_b2, lambda j: links.at(y=xor4(y, j)), node_grad
    )
    next(part_job)
    next(edge_job)
    next(node_job)
    next(total)
    next(part_job)
    next(node_job)
    next(edge_job)
    for _ in part_job:
        pass
    node_grad[...] = node_grad[...] + s.direct[:N] + s.recv_own[...]
    node_out = links.local(node_grad, s.node_grad)
    next(node_job)
    for _ in total:
        pass
    coarse_grad[...] = coarse_grad[...] + s.direct[N:]
    coarse_out = links.local(coarse_grad, s.coarse_grad)
    next(node_job)
    next(node_job)
    next(edge_job)
    for job in (node_job, edge_job):
        for _ in job:
            pass
    for copy in (edge_out, node_out, coarse_out):
        copy.wait()
    links.finish()


def finish(e_grad, n_grad, node_grad, coarse_grad, edge_grad, node_out, coarse_out, edge_out, ef, es, nf, ns, sems):
    copies = [
        pltpu.make_async_copy(src, dst, sems.at[k])
        for k, (src, dst) in enumerate(((edge_grad, edge_out), (coarse_grad, coarse_out), (node_grad, node_out)))
    ]
    for copy in copies:
        copy.start()
    for i in range(2 * RE // 16):
        row = i * 16
        core, block = row // RE, (row % RE) // 16
        out, at = (ef, row) if row < 384 else (es, row - 384)
        out[at : at + 16, :256] = e_grad[core, 2 * block].astype(F32)
        out[at : at + 16, 256:] = e_grad[core, 2 * block + 1].astype(F32)
    for i in range(2 * RN // ZR):
        row = i * ZR
        out, at = (nf, row) if row < 256 else (ns, row - 256)
        for j in range(NX):
            out[at : at + ZR, j * 128 : (j + 1) * 128] = n_grad[row // RN, j, (row % RN) // ZR].astype(F32)
    for copy in copies:
        copy.wait()


def program(
    node_lat, coarse_lat, edge_lat, senders, receivers, halo_rows, edge_live, edge_first, edge_second,
    node_first, node_second, edge_gain, node_gain, node_cotangent, coarse_cotangent, edge_cotangent,
):
    vmem = pl.BlockSpec(memory_space=pltpu.VMEM)
    anywhere = pl.BlockSpec(memory_space=pl.ANY)
    semaphores = [pltpu.SemaphoreType.DMA((count,)) for count in (SENDS, SENDS, LOCALS)]
    node_grad, coarse_grad, edge_grad, e_grad, n_grad = pl.pallas_call(
        body,
        out_shape=[jax.ShapeDtypeStruct(*v) for v in OUTPUTS.values()],
        in_specs=[vmem if small else anywhere for small in INPUTS.values()],
        out_specs=[anywhere] * len(OUTPUTS),
        scratch_shapes=[pltpu.VMEM(*v) for d in (SCRATCH, EDGE_JOB, NODE_JOB) for v in d.values()]
        + semaphores,
        compiler_params=pltpu.CompilerParams(
            collective_id=0, has_side_effects=True, vmem_limit_bytes=60 * 1024 * 1024
        ),
        name="layer",
    )(
        node_lat,
        coarse_lat,
        edge_lat,
        senders.reshape(1, E),
        receivers.reshape(1, E),
        halo_rows.T,
        edge_live.reshape(1, 1),
        edge_first,
        edge_second,
        node_first,
        node_second,
        edge_gain.reshape(1, D),
        node_gain.reshape(1, D),
        node_cotangent,
        coarse_cotangent,
        edge_cotangent,
    )
    shapes = [(N, D), (C, D), (E, D), (384, D), (128, D), (256, D), (128, D)]
    return pl.pallas_call(
        finish,
        out_shape=[jax.ShapeDtypeStruct(v, F32) for v in shapes],
        in_specs=[vmem, vmem, anywhere, anywhere, anywhere],
        out_specs=[anywhere] * 3 + [vmem] * 4,
        scratch_shapes=[pltpu.SemaphoreType.DMA((3,))],
        compiler_params=pltpu.CompilerParams(vmem_limit_bytes=60 * 1024 * 1024),
        name="finish",
    )(e_grad, n_grad, node_grad, coarse_grad, edge_grad)


def solution(mesh):
    rows = P(("graph", "feat"), None)
    return jax.shard_map(
        program,
        mesh=mesh,
        in_specs=(
            rows, P(), rows, P(("graph", "feat")), P(("graph", "feat")), rows, P(("graph", "feat")),
            P("feat", None), P("feat", None), P("feat", None), P("feat", None), P(), P(), rows, P(), rows,
        ),
        out_specs=(
            rows, P(), rows, P("feat", None), P("feat", None), P("feat", None), P("feat", None),
        ),
        check_vma=False,
    )
```

```python
import functools

import jax
import jax.numpy as jnp
from jax import lax
from jax.experimental import pallas as pl
from jax.experimental.pallas import tpu as pltpu
from jax.sharding import PartitionSpec as P

NORM_EPSILON = 1e-05
F32 = jnp.float32
BF16 = jnp.bfloat16
MESH = pl.DeviceIdType.MESH

D = 512
N = 128
E = 512
C = 256
NX, NY, NZ, NC = 4, 4, 8, 2
G = NX * NZ * NC
HALO = 8
RE, RN = 128, 192
ZR = 32
PLANE = NX * NZ


def dot(a, b):
    return jnp.dot(a, b, preferred_element_type=F32)


def dot_nt(a, b):
    return lax.dot_general(a, b, (((1,), (1,)), ((), ())), preferred_element_type=F32)


def dot_tn(a, b):
    return lax.dot_general(a, b, (((0,), (0,)), ((), ())), preferred_element_type=F32)


def xor4(v, j):
    return (v, v + 1 - 2 * (v % 2), (v + 2) % 4, 3 - v)[j]


def aligned(index, by):
    return pl.multiple_of(index, by)


def normalise(output):
    centred = output - jnp.mean(output, axis=1, keepdims=True)
    inverse = lax.rsqrt(jnp.mean(centred * centred, axis=1, keepdims=True) + NORM_EPSILON)
    return centred * inverse, inverse


def norm_backward(upstream, gain, normed, inverse):
    scaled = upstream * gain
    grad = inverse * (
        scaled
        - jnp.mean(scaled, axis=1, keepdims=True)
        - normed * jnp.mean(scaled * normed, axis=1, keepdims=True)
    )
    return grad.astype(BF16)


def silu_backward(grad_hidden, before):
    sigma = jax.nn.sigmoid(before)
    return (grad_hidden * sigma * (1.0 + before * (1.0 - sigma))).astype(BF16)


SCRATCH = dict(
    nodes=((NY, N, D), BF16),
    ef=((3 * D, D), BF16),
    es=((D, D), BF16),
    nf=((2 * D, D), BF16),
    ns=((D, D), BF16),
    halo_hot=((G * HALO, NY * N), BF16),
    halo_hot_t=((NY * N, G * HALO), BF16),
    send_hot=((E, 1280), BF16),
    send_hot_t=((1280, E), BF16),
    recv_hot=((E, N + C), BF16),
    recv_hot_t=((N + C, E), BF16),
    out_slots=((G, 16, 256), BF16),
    in_slots=((G, 16, 256), BF16),
    back_out=((G, 16, 256), BF16),
    back_in=((G, 16, 256), BF16),
    halo=((G * HALO, D), BF16),
    edge_in=((E, 3 * D), BF16),
    before=((E, D), F32),
    hidden=((E, D), BF16),
    normed=((E, D), F32),
    inverse=((E, 1), F32),
    lin=((E, D), BF16),
    gbefore=((E, D), BF16),
    gnext=((E, D), F32),
    moved=((E, D), BF16),
    node_in=((N + C, 2 * D), BF16),
    n_before=((N + C, D), F32),
    n_hidden=((N + C, D), BF16),
    n_normed=((N + C, D), F32),
    n_inverse=((N + C, 1), F32),
    n_lin=((N + C, D), BF16),
    n_gbefore=((N + C, D), BF16),
    direct=((N + C, D), F32),
    gagg=((N + C, D), BF16),
    coarse_total=((C, D), BF16),
    coarse_part=((C, D), F32),
    recv_own=((N, D), F32),
    part_grads=((NY * N, D), F32),
    a1_src=((32, 16, 256), BF16),
    a1_rs=((32, 16, 256), BF16),
    a1_z=((NZ, 16, 256), BF16),
    a1_ag=((32, 16, 256), BF16),
    a2_src=((32, 16, 256), BF16),
    a2_rs=((32, 16, 256), BF16),
    a2_z=((NZ, 16, 256), BF16),
    a2_ag=((32, 16, 256), BF16),
    v_node_cot=((N, D), BF16),
    v_coarse_cot=((C, D), BF16),
    v_edge_cot=((E, D), BF16),
    v_edge_grad=((E, D), F32),
    v_node_grad=((N, D), F32),
    v_coarse_grad=((C, D), F32),
    p_y=((NY, N, D), BF16),
    p_a1=((2, N // 2, D), BF16),
    p_b1=((2, N // 2, D), BF16),
    p_a2=((N // 2, D), BF16),
    p_b2=((N // 2, D), BF16),
)


def job_scratch(r):
    return dict(
        w=((NY, 2 * r, D), BF16),
        c=((NY, r, D), BF16),
        y=((NY, r, D), BF16),
        ya1=((2, r // 2, D), BF16),
        yb1=((2, r // 2, D), BF16),
        ya2=((r // 2, D), BF16),
        yb2=((r // 2, D), BF16),
        sum=((r, D), F32),
    )


EDGE_JOB, NODE_JOB = job_scratch(RE), job_scratch(RN)
EDGE_JOB.update(
    ps=((PLANE, 16, 128), BF16),
    pr=((PLANE, 16, 128), BF16),
    g=((PLANE, 16, 128), BF16),
)
NODE_JOB.update(
    x=((NX, RN, 128), BF16),
    xa1=((2, RN // 2, 128), BF16),
    xb1=((2, RN // 2, 128), BF16),
    xa2=((RN // 2, 128), BF16),
    xb2=((RN // 2, 128), BF16),
    zs=((NZ, ZR, 128), BF16),
    zr=((NZ, ZR, 128), BF16),
    g=((NX, NZ, ZR, 128), BF16),
    extra=((NC, NZ * ZR, D), F32),
)
SENDS, LOCALS = 87, 17

SMALL, LARGE = True, False
INPUTS = dict(
    node_lat=LARGE, coarse_lat=LARGE, edge_lat=LARGE, senders=SMALL, receivers=SMALL, halo_rows=SMALL,
    edge_live=SMALL, w_ef=LARGE, w_es=LARGE, w_nf=LARGE, w_ns=LARGE, edge_gain=SMALL, node_gain=SMALL,
    node_cot=LARGE, coarse_cot=LARGE, edge_cot=LARGE,
)
OUTPUTS = dict(
    node_grad=((N, D), F32),
    coarse_grad=((C, D), F32),
    edge_grad=((E, D), F32),
    ea_grad=((NC, PLANE, 16, 128), BF16),
    eb_grad=((NC, PLANE, 16, 128), BF16),
    n_grad=((NC, NX, NZ, ZR, 128), BF16),
)


class Refs(dict):
    __getattr__ = dict.__getitem__


class Links:
    def __init__(self, send_sems, recv_sems, local_sems):
        self.send_sems, self.recv_sems, self.used, self.sent = send_sems, recv_sems, 0, []
        self.local_sems, self.local_used = local_sems, 0
        graph = lax.axis_index("graph")
        self.g, self.y = graph, lax.axis_index("feat")
        self.c, self.z, self.x = graph % 2, (graph // 2) % 8, graph // 16

    def slot(self):
        self.used += 1
        return self.used - 1

    def at(self, x=None, y=None, z=None, c=None):
        x = self.x if x is None else x
        y = self.y if y is None else y
        z = self.z if z is None else z
        c = self.c if c is None else c
        return ((x * 8 + z) * 2 + c, y)

    def local(self, src, dst):
        copy = pltpu.make_async_copy(src, dst, self.local_sems.at[self.local_used])
        self.local_used += 1
        copy.start()
        return copy

    def send(self, src, dst, device):
        k = self.slot()
        copy = pltpu.make_async_remote_copy(
            src_ref=src,
            dst_ref=dst,
            send_sem=self.send_sems.at[k],
            recv_sem=self.recv_sems.at[k],
            device_id=device,
            device_id_type=MESH,
        )
        copy.start()
        self.sent.append(copy)
        return copy

    def send_many(self, count, peer, src, dst, whole):
        k = self.slot()

        def body(j, carry):
            index, device = peer(j)
            pltpu.make_async_remote_copy(
                src_ref=src(index),
                dst_ref=dst,
                send_sem=self.send_sems.at[k],
                recv_sem=self.recv_sems.at[k],
                device_id=device,
                device_id_type=MESH,
            ).start()
            return carry

        lax.fori_loop(1, count, body, 0)
        self.sent.append(("many", whole, k))

        def wait():
            pltpu.make_async_copy(whole, whole, self.recv_sems.at[k]).wait()

        return wait

    def finish(self):
        for copy in self.sent:
            if isinstance(copy, tuple):
                pltpu.make_async_copy(copy[1], copy[1], self.send_sems.at[copy[2]]).wait()
            else:
                copy.wait_send()


def to_slots(rows):
    rows = rows.reshape(G, HALO, D)
    return jnp.concatenate([rows[:, :, :256], rows[:, :, 256:]], axis=1).astype(BF16)


def from_slots(slots):
    slots = slots.astype(F32)
    rows = jnp.concatenate([slots[:, :8, :], slots[:, 8:, :]], axis=2)
    return rows.reshape(G * HALO, D).astype(BF16)


def halving(links, buf, half, ra1, rb1, ra2, rb2, partner, total_out):
    lo, hi = pl.ds(0, half), pl.ds(half, half)
    p1, p3 = partner(1), partner(3)
    a = links.send(buf.at[pl.ds(1, 2), lo], ra1, p1)
    b = links.send(buf.at[pl.ds(2, 2), hi], rb1, p3)
    yield
    a.wait_recv()
    buf[3, lo] = (buf[3, lo].astype(F32) + ra1[1].astype(F32)).astype(BF16)
    a = links.send(buf.at[3, lo], ra2, p3)
    b.wait_recv()
    buf[1, hi] = (buf[1, hi].astype(F32) + rb1[0].astype(F32)).astype(BF16)
    b = links.send(buf.at[1, hi], rb2, p1)
    total_out[lo] = buf[0, lo].astype(F32) + ra1[0].astype(F32)
    total_out[hi] = buf[0, hi].astype(F32) + rb1[1].astype(F32)
    yield
    a.wait_recv()
    total_out[lo] = total_out[lo] + ra2[...].astype(F32)
    b.wait_recv()
    total_out[hi] = total_out[hi] + rb2[...].astype(F32)


def coarse_sum(links, source, src, rs, zb, ag, out):
    me = (links.x * 4 + links.y) * 2 + links.c

    def peer(j):
        m = (me + j * 11) % 32
        return m, links.at(x=m // 8, y=(m // 2) % 4, c=m % 2)

    for i in range(32):
        src[i] = source[(i // 2) * 16 : (i // 2) * 16 + 16, (i % 2) * 256 : (i % 2) * 256 + 256].astype(BF16)
    wait = links.send_many(32, peer, lambda m: src.at[m], rs.at[me], rs.at[pl.ds(0, 31)])
    rs[me] = src[me]
    yield
    wait()
    zb[links.z] = jnp.sum(rs[...].astype(F32), axis=0).astype(BF16)

    def along(j):
        to = (links.z + j * 3) % 8
        return to, links.at(z=to)

    wait = links.send_many(8, along, lambda m: zb.at[links.z], zb.at[links.z], zb.at[pl.ds(0, 7)])
    yield
    wait()
    ag[me] = jnp.sum(zb[...].astype(F32), axis=0).astype(BF16)
    wait = links.send_many(32, peer, lambda m: ag.at[me], ag.at[me], ag.at[pl.ds(0, 31)])
    yield
    wait()
    for i in range(32):
        out[(i // 2) * 16 : (i // 2) * 16 + 16, (i % 2) * 256 : (i % 2) * 256 + 256] = ag[i].astype(out.dtype)


def weight_scatter(links, t, r, fill):
    w, cin, ybuf = t.w, t.c, t.y
    other = links.at(c=1 - links.c)
    theirs = pl.ds(aligned((1 - links.c) * r, 16), r)
    mine = pl.ds(aligned(links.c * r, 16), r)
    copies = {}
    for j in (2, 1, 3, 0):
        fill(j, xor4(links.y, j))
        copies[j] = links.send(w.at[j, theirs], cin.at[j], other)
    yield
    for j in (2, 1, 3, 0):
        copies[j].wait_recv()
        ybuf[j] = (w[j, mine].astype(F32) + cin[j].astype(F32)).astype(BF16)
    total = t.sum
    yield from halving(
        links, ybuf, r // 2, t.ya1, t.yb1, t.ya2, t.yb2,
        lambda j: links.at(y=xor4(links.y, j)), total,
    )


def edge_weights_sum(links, t, r, fill, out):
    yield from weight_scatter(links, t, r, fill)
    total, ps, pr, gathered = t.sum, t.ps, t.pr, t.g
    for i in range(PLANE):
        ps[i] = total[(i // 4) * 16 : (i // 4) * 16 + 16, (i % 4) * 128 : (i % 4) * 128 + 128].astype(BF16)
    me = links.x * NZ + links.z

    def peer(k):
        m = (me + k * 11) % PLANE
        return m, links.at(x=m // NZ, z=m % NZ)

    wait = links.send_many(PLANE, peer, lambda m: ps.at[m], pr.at[me], pr.at[pl.ds(0, PLANE - 1)])
    pr[me] = ps[me]
    yield
    wait()
    gathered[me] = jnp.sum(pr[...].astype(F32), axis=0).astype(BF16)
    wait = links.send_many(
        PLANE, peer, lambda m: gathered.at[me], gathered.at[me], gathered.at[pl.ds(0, PLANE - 1)]
    )
    yield
    wait()
    copy = links.send(gathered, out.at[links.c], links.at(c=1 - links.c))
    own = links.local(gathered, out.at[links.c])
    yield
    copy.wait_recv()
    own.wait()


def node_weights_sum(links, t, r, fill, out):
    yield from weight_scatter(links, t, r, fill)
    for j in range(4):
        t.x[j] = t.sum[:, pl.ds(aligned(xor4(links.x, j) * 128, 128), 128)].astype(BF16)
    sub = t.sum.at[:, pl.ds(0, 128)]
    yield from halving(
        links, t.x, r // 2, t.xa1, t.xb1, t.xa2, t.xb2, lambda j: links.at(x=xor4(links.x, j)), sub
    )
    blocks = r // ZR
    for i in range(NZ):
        t.zs[i] = sub[i * ZR : (i + 1) * ZR].astype(BF16) if i < blocks else jnp.zeros((ZR, 128), BF16)

    def along(j):
        to = (links.z + j * 3) % NZ
        return to, links.at(z=to)

    wait = links.send_many(NZ, along, lambda m: t.zs.at[m], t.zr.at[links.z], t.zr.at[pl.ds(0, NZ - 1)])
    t.zr[links.z] = t.zs[links.z]
    yield
    wait()
    own = t.g.at[links.x]
    extra = t.extra[
        links.c, pl.ds(aligned(links.z * ZR, ZR), ZR), pl.ds(aligned(links.x * 128, 128), 128)
    ]
    own[links.z] = (jnp.sum(t.zr[...].astype(F32), axis=0) + extra).astype(BF16)
    wait = links.send_many(NZ, along, lambda m: own.at[links.z], own.at[links.z], own.at[pl.ds(0, NZ - 1)])
    yield
    wait()
    x1, x2, x3 = xor4(links.x, 1), xor4(links.x, 2), xor4(links.x, 3)
    every, lo, hi = pl.ds(0, blocks), pl.ds(0, blocks // 2), pl.ds(blocks // 2, blocks // 2)
    mine = t.g.at[links.x, every]
    a = links.send(mine, mine, links.at(x=x1))
    b = links.send(mine, mine, links.at(x=x3))
    yield
    a.wait_recv()
    a = links.send(t.g.at[x1, lo], t.g.at[x1, lo], links.at(x=x3))
    b.wait_recv()
    b = links.send(t.g.at[x3, hi], t.g.at[x3, hi], links.at(x=x1))
    yield
    a.wait_recv()
    b.wait_recv()
    result = t.g.at[:, every]
    copy = links.send(result, out.at[links.c, :, every], links.at(c=1 - links.c))
    local = links.local(result, out.at[links.c, :, every])
    yield
    copy.wait_recv()
    local.wait()


def body(*refs):
    refs = iter(refs)
    s = Refs(zip([*INPUTS, *OUTPUTS, *SCRATCH], refs))
    ea_refs, eb_refs = Refs(zip(EDGE_JOB, refs)), Refs(zip(EDGE_JOB, refs))
    node_refs = Refs(zip(NODE_JOB, refs))
    links = Links(*refs)
    x, y, z, c, g = links.x, links.y, links.z, links.c, links.g
    y1, y2, y3 = xor4(y, 1), xor4(y, 2), xor4(y, 3)
    other = links.at(c=1 - c)
    ef, es, nf, ns = s.ef, s.es, s.nf, s.ns
    weights = {"ef": 384, "es": 128, "nf": 256, "ns": 128}
    nodes, edge_in, node_in = s.nodes, s.edge_in, s.node_in

    barrier = pltpu.get_barrier_semaphore()

    def greet_graph(j, carry):
        pl.semaphore_signal(barrier, inc=1, device_id=((g + j) % G, y), device_id_type=MESH)
        return carry

    def greet_plane(j, carry):
        k = j // 3
        device = links.at(x=k // 2, c=k % 2, y=(y + 1 + j % 3) % 4)
        pl.semaphore_signal(barrier, inc=1, device_id=device, device_id_type=MESH)
        return carry

    lax.fori_loop(1, G, greet_graph, 0)
    lax.fori_loop(0, 24, greet_plane, 0)
    early = [
        links.local(s.node_lat, nodes.at[y]),
        links.local(s.node_lat, node_in.at[pl.ds(0, N), pl.ds(0, D)]),
        links.local(s.coarse_lat, node_in.at[pl.ds(N, C), pl.ds(0, D)]),
        links.local(s.edge_lat, edge_in.at[:, pl.ds(0, D)]),
    ]
    for name, rows in weights.items():
        early.append(links.local(s["w_" + name], s[name].at[pl.ds(aligned(y * rows, 16), rows)]))
    for name in ("node_cot", "coarse_cot", "edge_cot"):
        early.append(links.local(s[name], s["v_" + name]))
    pl.semaphore_wait(barrier, G - 1 + 24)

    lo, hi = pl.ds(0, N // 2), pl.ds(N // 2, N // 2)
    lat = s.node_lat
    a_lo = links.send(lat.at[lo], nodes.at[y, lo], links.at(y=y1))
    b_hi = links.send(lat.at[hi], nodes.at[y, hi], links.at(y=y3))
    a_hi = links.send(lat.at[hi], nodes.at[y, hi], links.at(y=y1))
    b_lo = links.send(lat.at[lo], nodes.at[y, lo], links.at(y=y3))

    lanes = lax.broadcasted_iota(jnp.int32, (E, 128), 1)
    subs = lax.broadcasted_iota(jnp.int32, (128, E), 0)

    def hot(code_row, hot_ref, hot_t_ref, width):
        across = jnp.broadcast_to(code_row, (128, E))
        down = jnp.transpose(across)
        for j in range(width // 128):
            hot_ref[:, j * 128 : (j + 1) * 128] = jnp.where(down == lanes + j * 128, 1.0, 0.0).astype(BF16)
            hot_t_ref[j * 128 : (j + 1) * 128, :] = jnp.where(across == subs + j * 128, 1.0, 0.0).astype(BF16)

    codes = s.halo_rows[...]
    spread = (
        lax.broadcasted_iota(jnp.int32, (G, G * HALO), 0)
        == lax.broadcasted_iota(jnp.int32, (G, G * HALO), 1) // HALO
    )
    spread = jnp.where(spread, 1.0, 0.0).astype(BF16)
    high = dot((codes // 16).astype(F32).astype(BF16), spread)
    low = dot((codes % 16).astype(F32).astype(BF16), spread)
    shape = (HALO, G * HALO)
    at_k = lax.broadcasted_iota(jnp.int32, shape, 0) == lax.broadcasted_iota(jnp.int32, shape, 1) % HALO
    codes = jnp.sum(jnp.where(at_k, high * 16.0 + low, 0.0), axis=0, keepdims=True).astype(jnp.int32)
    hot(codes, s.halo_hot, s.halo_hot_t, NY * N)
    for copy in early:
        copy.wait()

    a_lo.wait_recv()
    a2 = links.send(nodes.at[y1, lo], nodes.at[y1, lo], links.at(y=y3))
    b_hi.wait_recv()
    b2 = links.send(nodes.at[y3, hi], nodes.at[y3, hi], links.at(y=y1))

    def weight_rows(name, owner, first, count):
        rows = weights[name]
        return s[name].at[pl.ds(aligned(owner * rows + c * (rows // 2) + first, 16), count)]

    def weight_step1(group):
        copies = []
        for name in group:
            half = weights[name] // 2
            src = s["w_" + name].at[pl.ds(aligned(c * half, 16), half)]
            copies.append(
                (
                    name,
                    links.send(src, weight_rows(name, y, 0, half), links.at(y=y1)),
                    links.send(src, weight_rows(name, y, 0, half), links.at(y=y3)),
                )
            )
        return copies

    def weight_step2(copies):
        forward, swap = [], []
        for name, first, second in copies:
            half, quarter = weights[name] // 2, weights[name] // 4
            first.wait_recv()
            src = weight_rows(name, y1, 0, quarter)
            forward.append(links.send(src, src, links.at(y=y3)))
            src = weight_rows(name, y1, 0, half)
            swap.append(links.send(src, src, other))
            second.wait_recv()
            src = weight_rows(name, y3, quarter, quarter)
            forward.append(links.send(src, src, links.at(y=y1)))
            src = weight_rows(name, y3, 0, half)
            swap.append(links.send(src, src, other))
        return forward, swap

    def weight_step3(group, forward, swap):
        for copy in forward:
            copy.wait_recv()
        for name in group:
            src = weight_rows(name, y2, 0, weights[name] // 2)
            swap.append(links.send(src, src, other))
        return swap

    for copy in (a_hi, b_lo, a2, b2):
        copy.wait_recv()
    edge_weights = weight_step1(("ef", "es"))

    out_slots, in_slots = s.out_slots, s.in_slots
    part_nodes = nodes[...].reshape(NY * N, D)
    out_slots[...] = to_slots(dot(s.halo_hot[...], part_nodes))

    def graph_peer(j):
        to = (g + j * 29) % G
        return to, (to, y)

    halo_wait = links.send_many(
        G, graph_peer, lambda m: out_slots.at[m], in_slots.at[g], in_slots.at[pl.ds(0, G - 1)]
    )
    in_slots[g] = out_slots[g]

    live = s.edge_live[...]
    alive_row = lax.broadcasted_iota(jnp.int32, (1, E), 1) < live
    hot(jnp.where(alive_row, s.senders[...], -1), s.send_hot, s.send_hot_t, 1280)
    hot(jnp.where(alive_row, s.receivers[...], -1), s.recv_hot, s.recv_hot_t, N + C)
    node_lat, coarse_lat = node_in[:N, :D], node_in[N:, :D]
    edge_in[:, 2 * D :] = (
        dot(s.recv_hot[:, :N], node_lat) + dot(s.recv_hot[:, N:], coarse_lat)
    ).astype(BF16)
    edge_in[:, D : 2 * D] = (
        dot(s.send_hot[:, :512], part_nodes) + dot(s.send_hot[:, 1024:], coarse_lat)
    ).astype(BF16)
    edge_forward, edge_swap = weight_step2(edge_weights)
    node_weights = weight_step1(("nf", "ns"))
    edge_swap = weight_step3(("ef", "es"), edge_forward, edge_swap)
    for copy in edge_swap:
        copy.wait_recv()
    before = s.before
    before[...] = dot(edge_in[:, :D], ef[:D]) + dot(edge_in[:, 2 * D :], ef[2 * D :])

    node_forward, node_swap = weight_step2(node_weights)

    halo_wait()
    s.halo[...] = from_slots(in_slots[...])
    edge_in[:, D : 2 * D] = (
        edge_in[:, D : 2 * D].astype(F32) + dot(s.send_hot[:, 512:1024], s.halo[...])
    ).astype(BF16)
    before[...] = before[...] + dot(edge_in[:, D : 2 * D], ef[D : 2 * D])
    s.hidden[...] = (before[...] * jax.nn.sigmoid(before[...])).astype(BF16)
    normed, inverse = normalise(dot(s.hidden[...], es[...]))
    s.normed[...] = normed
    s.inverse[...] = inverse
    edge_next = (edge_in[:, :D].astype(F32) + normed * s.edge_gain[...]).astype(BF16)
    s.coarse_part[...] = dot(s.recv_hot_t[N:], edge_next)
    total = coarse_sum(
        links, s.coarse_part, s.a1_src, s.a1_rs, s.a1_z, s.a1_ag, s.coarse_total
    )
    next(total)
    own_agg = dot(s.recv_hot_t[:N], edge_next).astype(BF16)
    node_in[:N, D:] = own_agg
    node_swap = weight_step3(("nf", "ns"), node_forward, node_swap)

    def node_up(rows):
        name = "v_node_cot" if rows.start == 0 else "v_coarse_cot"
        return s[name][...].astype(F32)

    def node_pass_forward(rows):
        a = dot(node_in[rows], nf[...])
        hidden = (a * jax.nn.sigmoid(a)).astype(BF16)
        s.n_before[rows] = a
        s.n_hidden[rows] = hidden
        n, inv = normalise(dot(hidden, ns[...]))
        s.n_normed[rows] = n
        s.n_inverse[rows] = inv

    def node_pass_backward(rows):
        up = node_up(rows)
        q = norm_backward(up, s.node_gain[...], s.n_normed[rows], s.n_inverse[rows])
        zz = silu_backward(dot_nt(q, ns[...]), s.n_before[rows])
        s.n_lin[rows] = q
        s.n_gbefore[rows] = zz
        s.direct[rows] = up + dot_nt(zz, nf[:D])
        s.gagg[rows] = dot_nt(zz, nf[D:]).astype(BF16)

    own, coarse = slice(0, N), slice(N, N + C)

    def fill_node(j, to):
        w = node_refs.w
        w[j, :256] = dot_tn(node_in[:N, pl.ds(aligned(to * 256, 128), 256)], s.n_gbefore[:N]).astype(BF16)
        w[j, 256:] = dot_tn(s.n_hidden[:N, pl.ds(aligned(to * 128, 128), 128)], s.n_lin[:N]).astype(BF16)

    node_job = node_weights_sum(links, node_refs, RN, fill_node, s.n_grad)
    next(total)
    for copy in node_swap:
        copy.wait_recv()
    node_pass_forward(own)
    node_pass_backward(own)
    next(node_job)
    next(total)
    next(node_job)
    for _ in total:
        pass
    node_in[N:, D:] = s.coarse_total[...]
    node_pass_forward(coarse)
    node_pass_backward(coarse)

    s.gnext[...] = s.v_edge_cot[...].astype(F32) + dot(s.recv_hot[...], s.gagg[...])
    alive = lax.broadcasted_iota(jnp.int32, (E, 1), 0) < live
    upstream = jnp.where(alive, s.gnext[...], 0.0)
    q = norm_backward(upstream, s.edge_gain[...], s.normed[...], s.inverse[...])
    s.lin[...] = q
    s.gbefore[...] = silu_backward(dot_nt(q, es[...]), before[...])
    gbefore = s.gbefore

    next(node_job)

    def fill_ea(j, to):
        ea_refs.w[j] = dot_tn(edge_in[:, pl.ds(aligned(to * 384, 128), 256)], gbefore[...]).astype(BF16)

    def fill_eb(j, to):
        first = dot_tn(edge_in[:, pl.ds(aligned(to * 384 + 256, 128), 128)], gbefore[...])
        second = dot_tn(s.hidden[:, pl.ds(aligned(to * 128, 128), 128)], s.lin[...])
        eb_refs.w[j, :128] = first.astype(BF16)
        eb_refs.w[j, 128:] = second.astype(BF16)

    ea_job = edge_weights_sum(links, ea_refs, RE, fill_ea, s.ea_grad)
    eb_job = edge_weights_sum(links, eb_refs, RE, fill_eb, s.eb_grad)
    next(ea_job)
    next(eb_job)
    moved = s.moved
    moved[...] = dot_nt(gbefore[...], ef[D : 2 * D]).astype(BF16)
    back_out, back_in = s.back_out, s.back_in
    back_out[...] = to_slots(dot(s.send_hot_t[512:1024], moved[...]))
    back_wait = links.send_many(
        G, graph_peer, lambda m: back_out.at[m], back_in.at[g], back_in.at[pl.ds(0, G - 1)]
    )
    back_in[g] = back_out[g]
    next(ea_job)
    next(eb_job)
    next(node_job)
    s.part_grads[...] = dot(s.send_hot_t[:512], moved[...])
    s.coarse_part[...] = dot(s.send_hot_t[1024:], moved[...])
    moved[...] = dot_nt(gbefore[...], ef[2 * D :]).astype(BF16)
    s.coarse_part[...] = s.coarse_part[...] + dot(s.recv_hot_t[N:], moved[...])
    coarse_grad = s.v_coarse_grad
    total = coarse_sum(links, s.coarse_part, s.a2_src, s.a2_rs, s.a2_z, s.a2_ag, coarse_grad)
    next(total)
    s.recv_own[...] = dot(s.recv_hot_t[:N], moved[...])
    s.v_edge_grad[...] = s.gnext[...] + dot_nt(gbefore[...], ef[:D])
    edge_out = links.local(s.v_edge_grad, s.edge_grad)
    next(ea_job)
    next(node_job)
    extra = node_refs.extra
    first = dot_tn(node_in[N:, pl.ds(aligned(y * 256, 128), 256)], s.n_gbefore[N:])
    extra[0, :RN] = first[:RN]
    extra[1, : 256 - RN] = first[RN:]
    extra[1, 256 - RN : RN] = dot_tn(s.n_hidden[N:, pl.ds(aligned(y * 128, 128), 128)], s.n_lin[N:])
    extra[:, RN:] = jnp.zeros((NC, NZ * ZR - RN, D), F32)
    next(eb_job)
    next(total)
    next(node_job)
    next(ea_job)
    next(eb_job)
    next(node_job)
    next(total)

    back_wait()
    s.halo[...] = from_slots(back_in[...])
    s.part_grads[...] = s.part_grads[...] + dot(s.halo_hot_t[...], s.halo[...])
    p_y = s.p_y
    for j in range(4):
        p_y[j] = s.part_grads[pl.ds(aligned(xor4(y, j) * N, 16), N), :].astype(BF16)
    node_grad = s.v_node_grad
    part_job = halving(
        links, p_y, N // 2, s.p_a1, s.p_b1, s.p_a2, s.p_b2, lambda j: links.at(y=xor4(y, j)), node_grad
    )
    next(part_job)
    next(ea_job)
    next(node_job)
    next(eb_job)
    next(part_job)
    next(node_job)
    for _ in total:
        pass
    coarse_grad[...] = coarse_grad[...] + s.direct[N:]
    coarse_out = links.local(coarse_grad, s.coarse_grad)
    next(ea_job)
    for _ in part_job:
        pass
    node_grad[...] = node_grad[...] + s.direct[:N] + s.recv_own[...]
    node_out = links.local(node_grad, s.node_grad)
    next(node_job)
    next(eb_job)
    for job in (ea_job, node_job, eb_job):
        for _ in job:
            pass
    for copy in (edge_out, node_out, coarse_out):
        copy.wait()
    links.finish()


def finish(ea_grad, eb_grad, n_grad, node_grad, coarse_grad, edge_grad, node_out, coarse_out, edge_out, ef, es, nf, ns, sems):
    copies = [
        pltpu.make_async_copy(src, dst, sems.at[k])
        for k, (src, dst) in enumerate(((edge_grad, edge_out), (coarse_grad, coarse_out), (node_grad, node_out)))
    ]
    for copy in copies:
        copy.start()
    for i in range(4 * RE // 16):
        row = i * 16
        pieces, core, block = (ea_grad, eb_grad)[i // 16], (i // 8) % 2, i % 8
        out, at = (ef, row) if row < 384 else (es, row - 384)
        for j in range(4):
            out[at : at + 16, j * 128 : (j + 1) * 128] = pieces[core, 4 * block + j].astype(F32)
    for i in range(2 * RN // ZR):
        row = i * ZR
        out, at = (nf, row) if row < 256 else (ns, row - 256)
        for j in range(NX):
            out[at : at + ZR, j * 128 : (j + 1) * 128] = n_grad[row // RN, j, (row % RN) // ZR].astype(F32)
    for copy in copies:
        copy.wait()


def program(
    node_lat, coarse_lat, edge_lat, senders, receivers, halo_rows, edge_live, edge_first, edge_second,
    node_first, node_second, edge_gain, node_gain, node_cotangent, coarse_cotangent, edge_cotangent,
):
    vmem = pl.BlockSpec(memory_space=pltpu.VMEM)
    anywhere = pl.BlockSpec(memory_space=pl.ANY)
    semaphores = [pltpu.SemaphoreType.DMA((count,)) for count in (SENDS, SENDS, LOCALS)]
    node_grad, coarse_grad, edge_grad, ea_grad, eb_grad, n_grad = pl.pallas_call(
        body,
        out_shape=[jax.ShapeDtypeStruct(*v) for v in OUTPUTS.values()],
        in_specs=[vmem if small else anywhere for small in INPUTS.values()],
        out_specs=[anywhere] * len(OUTPUTS),
        scratch_shapes=[pltpu.VMEM(*v) for d in (SCRATCH, EDGE_JOB, EDGE_JOB, NODE_JOB) for v in d.values()]
        + semaphores,
        compiler_params=pltpu.CompilerParams(
            collective_id=0, has_side_effects=True, vmem_limit_bytes=60 * 1024 * 1024
        ),
        name="layer",
    )(
        node_lat,
        coarse_lat,
        edge_lat,
        senders.reshape(1, E),
        receivers.reshape(1, E),
        halo_rows.T,
        edge_live.reshape(1, 1),
        edge_first,
        edge_second,
        node_first,
        node_second,
        edge_gain.reshape(1, D),
        node_gain.reshape(1, D),
        node_cotangent,
        coarse_cotangent,
        edge_cotangent,
    )
    shapes = [(N, D), (C, D), (E, D), (384, D), (128, D), (256, D), (128, D)]
    return pl.pallas_call(
        finish,
        out_shape=[jax.ShapeDtypeStruct(v, F32) for v in shapes],
        in_specs=[vmem] * 6,
        out_specs=[anywhere] * 3 + [vmem] * 4,
        scratch_shapes=[pltpu.SemaphoreType.DMA((3,))],
        compiler_params=pltpu.CompilerParams(vmem_limit_bytes=60 * 1024 * 1024),
        name="finish",
    )(ea_grad, eb_grad, n_grad, node_grad, coarse_grad, edge_grad)


def solution(mesh):
    rows = P(("graph", "feat"), None)
    return jax.shard_map(
        program,
        mesh=mesh,
        in_specs=(
            rows, P(), rows, P(("graph", "feat")), P(("graph", "feat")), rows, P(("graph", "feat")),
            P("feat", None), P("feat", None), P("feat", None), P("feat", None), P(), P(), rows, P(), rows,
        ),
        out_specs=(
            rows, P(), rows, P("feat", None), P("feat", None), P("feat", None), P("feat", None),
        ),
        check_vma=False,
    )
```

```python
import functools

import jax
import jax.numpy as jnp
from jax import lax
from jax.experimental import pallas as pl
from jax.experimental.pallas import tpu as pltpu
from jax.sharding import PartitionSpec as P

NORM_EPSILON = 1e-05
F32 = jnp.float32
BF16 = jnp.bfloat16
MESH = pl.DeviceIdType.MESH

D = 512
N = 128
E = 512
C = 256
NX, NY, NZ, NC = 4, 4, 8, 2
G = NX * NZ * NC
HALO = 8
RE, RN = 128, 192
ZR = 32
PLANE = NX * NZ


def dot(a, b):
    return jnp.dot(a, b, preferred_element_type=F32)


def dot_nt(a, b):
    return lax.dot_general(a, b, (((1,), (1,)), ((), ())), preferred_element_type=F32)


def dot_tn(a, b):
    return lax.dot_general(a, b, (((0,), (0,)), ((), ())), preferred_element_type=F32)


def xor4(v, j):
    return (v, v + 1 - 2 * (v % 2), (v + 2) % 4, 3 - v)[j]


def aligned(index, by):
    return pl.multiple_of(index, by)


def normalise(output):
    centred = output - jnp.mean(output, axis=1, keepdims=True)
    inverse = lax.rsqrt(jnp.mean(centred * centred, axis=1, keepdims=True) + NORM_EPSILON)
    return centred * inverse, inverse


def norm_backward(upstream, gain, normed, inverse):
    scaled = upstream * gain
    grad = inverse * (
        scaled
        - jnp.mean(scaled, axis=1, keepdims=True)
        - normed * jnp.mean(scaled * normed, axis=1, keepdims=True)
    )
    return grad.astype(BF16)


def silu_backward(grad_hidden, before):
    sigma = jax.nn.sigmoid(before)
    return (grad_hidden * sigma * (1.0 + before * (1.0 - sigma))).astype(BF16)


SCRATCH = dict(
    nodes=((NY, N, D), BF16),
    ef=((3 * D, D), BF16),
    es=((D, D), BF16),
    nf=((2 * D, D), BF16),
    ns=((D, D), BF16),
    halo_hot=((G * HALO, NY * N), BF16),
    halo_hot_t=((NY * N, G * HALO), BF16),
    send_hot=((E, 1280), BF16),
    send_hot_t=((1280, E), BF16),
    recv_hot=((E, N + C), BF16),
    recv_hot_t=((N + C, E), BF16),
    out_slots=((G, 16, 256), BF16),
    in_slots=((G, 16, 256), BF16),
    back_out=((G, 16, 256), BF16),
    back_in=((G, 16, 256), BF16),
    halo=((G * HALO, D), BF16),
    edge_in=((E, 3 * D), BF16),
    edge_in_t=((3 * D, E), BF16),
    hidden_t=((D, E), BF16),
    before=((E, D), F32),
    hidden=((E, D), BF16),
    normed=((E, D), F32),
    inverse=((E, 1), F32),
    lin=((E, D), BF16),
    gbefore=((E, D), BF16),
    gnext=((E, D), F32),
    moved=((E, D), BF16),
    node_in=((N + C, 2 * D), BF16),
    n_before=((N + C, D), F32),
    n_hidden=((N + C, D), BF16),
    n_normed=((N + C, D), F32),
    n_inverse=((N + C, 1), F32),
    n_lin=((N + C, D), BF16),
    n_gbefore=((N + C, D), BF16),
    direct=((N + C, D), F32),
    gagg=((N + C, D), BF16),
    coarse_total=((C, D), BF16),
    coarse_part=((C, D), F32),
    recv_own=((N, D), F32),
    part_grads=((NY * N, D), F32),
    a1_src=((32, 16, 256), BF16),
    a1_rs=((32, 16, 256), BF16),
    a1_z=((NZ, 16, 256), BF16),
    a1_ag=((32, 16, 256), BF16),
    a2_src=((32, 16, 256), BF16),
    a2_rs=((32, 16, 256), BF16),
    a2_z=((NZ, 16, 256), BF16),
    a2_ag=((32, 16, 256), BF16),
    v_halo_rows=((HALO, G), jnp.int32),
    v_senders=((1, E), jnp.int32),
    v_receivers=((1, E), jnp.int32),
    v_edge_gain=((1, D), F32),
    v_node_gain=((1, D), F32),
    v_node_cot=((N, D), BF16),
    v_coarse_cot=((C, D), BF16),
    v_edge_cot=((E, D), BF16),
    p_y=((NY, N, D), BF16),
    p_a1=((2, N // 2, D), BF16),
    p_b1=((2, N // 2, D), BF16),
    p_a2=((N // 2, D), BF16),
    p_b2=((N // 2, D), BF16),
)


def job_scratch(r):
    return dict(
        w=((NY, 2 * r, D), BF16),
        c=((NY, r, D), BF16),
        y=((NY, r, D), BF16),
        ya1=((2, r // 2, D), BF16),
        yb1=((2, r // 2, D), BF16),
        ya2=((r // 2, D), BF16),
        yb2=((r // 2, D), BF16),
        sum=((r, D), F32),
    )


EDGE_JOB, NODE_JOB = job_scratch(RE), job_scratch(RN)
EDGE_JOB.update(
    ps=((PLANE, 16, 128), BF16),
    pr=((PLANE, 16, 128), BF16),
    g=((PLANE, 16, 128), BF16),
)
NODE_JOB.update(
    x=((NX, RN, 128), BF16),
    xr=((NX, RN, 128), BF16),
    zs=((NZ, ZR, 128), BF16),
    zr=((NZ, ZR, 128), BF16),
    g=((NX, NZ, ZR, 128), BF16),
    extra=((NC, NZ * ZR, D), F32),
)
SENDS, LOCALS = 81, 17

INPUTS = (
    "node_lat", "coarse_lat", "edge_lat", "senders", "receivers", "halo_rows", "edge_live", "w_ef", "w_es",
    "w_nf", "w_ns", "edge_gain", "node_gain", "node_cot", "coarse_cot", "edge_cot",
)
OUTPUTS = dict(
    node_grad=((N, D), F32),
    coarse_grad=((C, D), F32),
    edge_grad=((E, D), F32),
    ea_grad=((NC, PLANE, 16, 128), BF16),
    eb_grad=((NC, PLANE, 16, 128), BF16),
    n_grad=((NC, NX, NZ, ZR, 128), BF16),
)


class Refs(dict):
    __getattr__ = dict.__getitem__


class Links:
    def __init__(self, send_sems, recv_sems, local_sems):
        self.send_sems, self.recv_sems, self.used, self.sent = send_sems, recv_sems, 0, []
        self.local_sems, self.local_used = local_sems, 0
        graph = lax.axis_index("graph")
        self.g, self.y = graph, lax.axis_index("feat")
        self.c, self.z, self.x = graph % 2, (graph // 2) % 8, graph // 16

    def slot(self):
        self.used += 1
        return self.used - 1

    def at(self, x=None, y=None, z=None, c=None):
        x = self.x if x is None else x
        y = self.y if y is None else y
        z = self.z if z is None else z
        c = self.c if c is None else c
        return ((x * 8 + z) * 2 + c, y)

    def local(self, src, dst):
        copy = pltpu.make_async_copy(src, dst, self.local_sems.at[self.local_used])
        self.local_used += 1
        copy.start()
        return copy

    def send(self, src, dst, device):
        k = self.slot()
        copy = pltpu.make_async_remote_copy(
            src_ref=src,
            dst_ref=dst,
            send_sem=self.send_sems.at[k],
            recv_sem=self.recv_sems.at[k],
            device_id=device,
            device_id_type=MESH,
        )
        copy.start()
        self.sent.append(copy)
        return copy

    def send_many(self, count, peer, src, dst, whole):
        k = self.slot()

        def body(j, carry):
            index, device = peer(j)
            pltpu.make_async_remote_copy(
                src_ref=src(index),
                dst_ref=dst,
                send_sem=self.send_sems.at[k],
                recv_sem=self.recv_sems.at[k],
                device_id=device,
                device_id_type=MESH,
            ).start()
            return carry

        lax.fori_loop(1, count, body, 0)
        self.sent.append(("many", whole, k))

        def wait():
            pltpu.make_async_copy(whole, whole, self.recv_sems.at[k]).wait()

        return wait

    def finish(self):
        for copy in self.sent:
            if isinstance(copy, tuple):
                pltpu.make_async_copy(copy[1], copy[1], self.send_sems.at[copy[2]]).wait()
            else:
                copy.wait_send()


def to_slots(rows):
    rows = rows.reshape(G, HALO, D)
    return jnp.concatenate([rows[:, :, :256], rows[:, :, 256:]], axis=1).astype(BF16)


def from_slots(slots):
    slots = slots.astype(F32)
    rows = jnp.concatenate([slots[:, :8, :], slots[:, 8:, :]], axis=2)
    return rows.reshape(G * HALO, D).astype(BF16)


def halving(links, buf, half, ra1, rb1, ra2, rb2, partner, total_out):
    lo, hi = pl.ds(0, half), pl.ds(half, half)
    p1, p3 = partner(1), partner(3)
    a = links.send(buf.at[pl.ds(1, 2), lo], ra1, p1)
    b = links.send(buf.at[pl.ds(2, 2), hi], rb1, p3)
    yield
    a.wait_recv()
    buf[3, lo] = (buf[3, lo].astype(F32) + ra1[1].astype(F32)).astype(BF16)
    a = links.send(buf.at[3, lo], ra2, p3)
    b.wait_recv()
    buf[1, hi] = (buf[1, hi].astype(F32) + rb1[0].astype(F32)).astype(BF16)
    b = links.send(buf.at[1, hi], rb2, p1)
    total_out[lo] = buf[0, lo].astype(F32) + ra1[0].astype(F32)
    total_out[hi] = buf[0, hi].astype(F32) + rb1[1].astype(F32)
    yield
    a.wait_recv()
    total_out[lo] = total_out[lo] + ra2[...].astype(F32)
    b.wait_recv()
    total_out[hi] = total_out[hi] + rb2[...].astype(F32)


def coarse_sum(links, source, src, rs, zb, ag, out):
    me = (links.x * 4 + links.y) * 2 + links.c

    def peer(j):
        m = (me + j * 11) % 32
        return m, links.at(x=m // 8, y=(m // 2) % 4, c=m % 2)

    for i in range(32):
        src[i] = source[(i // 2) * 16 : (i // 2) * 16 + 16, (i % 2) * 256 : (i % 2) * 256 + 256].astype(BF16)
    wait = links.send_many(32, peer, lambda m: src.at[m], rs.at[me], rs.at[pl.ds(0, 31)])
    rs[me] = src[me]
    yield
    wait()
    zb[links.z] = jnp.sum(rs[...].astype(F32), axis=0).astype(BF16)

    def along(j):
        to = (links.z + j * 3) % 8
        return to, links.at(z=to)

    wait = links.send_many(8, along, lambda m: zb.at[links.z], zb.at[links.z], zb.at[pl.ds(0, 7)])
    yield
    wait()
    ag[me] = jnp.sum(zb[...].astype(F32), axis=0).astype(BF16)
    wait = links.send_many(32, peer, lambda m: ag.at[me], ag.at[me], ag.at[pl.ds(0, 31)])
    yield
    wait()
    for i in range(32):
        out[(i // 2) * 16 : (i // 2) * 16 + 16, (i % 2) * 256 : (i % 2) * 256 + 256] = ag[i].astype(out.dtype)


def weight_scatter(links, t, r, fill):
    w, cin, ybuf = t.w, t.c, t.y
    other = links.at(c=1 - links.c)
    theirs = pl.ds(aligned((1 - links.c) * r, 16), r)
    mine = pl.ds(aligned(links.c * r, 16), r)
    copies = {}
    for j in (2, 1, 3, 0):
        fill(j, xor4(links.y, j))
        copies[j] = links.send(w.at[j, theirs], cin.at[j], other)
    yield
    for j in (2, 1, 3, 0):
        copies[j].wait_recv()
        ybuf[j] = (w[j, mine].astype(F32) + cin[j].astype(F32)).astype(BF16)
    total = t.sum
    yield from halving(
        links, ybuf, r // 2, t.ya1, t.yb1, t.ya2, t.yb2,
        lambda j: links.at(y=xor4(links.y, j)), total,
    )


def edge_weights_sum(links, t, r, fill, out):
    yield from weight_scatter(links, t, r, fill)
    total, ps, pr, gathered = t.sum, t.ps, t.pr, t.g
    for i in range(PLANE):
        ps[i] = total[(i // 4) * 16 : (i // 4) * 16 + 16, (i % 4) * 128 : (i % 4) * 128 + 128].astype(BF16)
    me = links.x * NZ + links.z

    def peer(k):
        m = (me + k * 11) % PLANE
        return m, links.at(x=m // NZ, z=m % NZ)

    wait = links.send_many(PLANE, peer, lambda m: ps.at[m], pr.at[me], pr.at[pl.ds(0, PLANE - 1)])
    pr[me] = ps[me]
    yield
    wait()
    gathered[me] = jnp.sum(pr[...].astype(F32), axis=0).astype(BF16)
    wait = links.send_many(
        PLANE, peer, lambda m: gathered.at[me], gathered.at[me], gathered.at[pl.ds(0, PLANE - 1)]
    )
    yield
    wait()
    copy = links.send(gathered, out.at[links.c], links.at(c=1 - links.c))
    out[links.c] = gathered[...]
    yield
    copy.wait_recv()


def node_weights_sum(links, t, r, fill, out):
    yield from weight_scatter(links, t, r, fill)
    for j in range(NX):
        t.x[j] = t.sum[:, j * 128 : (j + 1) * 128].astype(BF16)

    def across(j):
        to = (links.x + j) % NX
        return to, links.at(x=to)

    wait = links.send_many(NX, across, lambda m: t.x.at[m], t.xr.at[links.x], t.xr.at[pl.ds(0, NX - 1)])
    t.xr[links.x] = t.x[links.x]
    yield
    wait()
    sub = jnp.sum(t.xr[...].astype(F32), axis=0)
    blocks = r // ZR
    for i in range(NZ):
        t.zs[i] = sub[i * ZR : (i + 1) * ZR].astype(BF16) if i < blocks else jnp.zeros((ZR, 128), BF16)

    def along(j):
        to = (links.z + j * 3) % NZ
        return to, links.at(z=to)

    wait = links.send_many(NZ, along, lambda m: t.zs.at[m], t.zr.at[links.z], t.zr.at[pl.ds(0, NZ - 1)])
    t.zr[links.z] = t.zs[links.z]
    yield
    wait()
    own = t.g.at[links.x]
    extra = t.extra[
        links.c, pl.ds(aligned(links.z * ZR, ZR), ZR), pl.ds(aligned(links.x * 128, 128), 128)
    ]
    own[links.z] = (jnp.sum(t.zr[...].astype(F32), axis=0) + extra).astype(BF16)
    wait = links.send_many(NZ, along, lambda m: own.at[links.z], own.at[links.z], own.at[pl.ds(0, NZ - 1)])
    yield
    wait()
    every = pl.ds(0, blocks)
    mine = t.g.at[links.x, every]
    wait = links.send_many(NX, across, lambda m: mine, mine, t.g.at[pl.ds(0, NX - 1), every])
    yield
    wait()
    result = t.g.at[:, every]
    copy = links.send(result, out.at[links.c, :, every], links.at(c=1 - links.c))
    out[links.c] = t.g[...]
    yield
    copy.wait_recv()


def body(*refs):
    refs = iter(refs)
    s = Refs(zip([*INPUTS, *OUTPUTS, *SCRATCH], refs))
    ea_refs, eb_refs = Refs(zip(EDGE_JOB, refs)), Refs(zip(EDGE_JOB, refs))
    node_refs = Refs(zip(NODE_JOB, refs))
    s.update(live=next(refs))
    links = Links(*refs)
    x, y, z, c, g = links.x, links.y, links.z, links.c, links.g
    y1, y2, y3 = xor4(y, 1), xor4(y, 2), xor4(y, 3)
    other = links.at(c=1 - c)
    ef, es, nf, ns = s.ef, s.es, s.nf, s.ns
    weights = {"ef": 384, "es": 128, "nf": 256, "ns": 128}
    nodes, edge_in, node_in = s.nodes, s.edge_in, s.node_in

    barrier = pltpu.get_barrier_semaphore()

    def greet_graph(j, carry):
        pl.semaphore_signal(barrier, inc=1, device_id=((g + j) % G, y), device_id_type=MESH)
        return carry

    def greet_plane(j, carry):
        k = j // 3
        device = links.at(x=k // 2, c=k % 2, y=(y + 1 + j % 3) % 4)
        pl.semaphore_signal(barrier, inc=1, device_id=device, device_id_type=MESH)
        return carry

    lax.fori_loop(1, G, greet_graph, 0)
    lax.fori_loop(0, 24, greet_plane, 0)
    live_copy = links.local(s.edge_live, s.live)
    codes_copies = [links.local(s[name], s["v_" + name]) for name in ("halo_rows", "senders", "receivers")]
    gain_copies = [links.local(s[name], s["v_" + name]) for name in ("edge_gain", "node_gain")]
    early = [
        links.local(s.node_lat, nodes.at[y]),
        links.local(s.node_lat, node_in.at[pl.ds(0, N), pl.ds(0, D)]),
        links.local(s.coarse_lat, node_in.at[pl.ds(N, C), pl.ds(0, D)]),
        links.local(s.edge_lat, edge_in.at[:, pl.ds(0, D)]),
    ]
    for name, rows in weights.items():
        early.append(links.local(s["w_" + name], s[name].at[pl.ds(aligned(y * rows, 16), rows)]))
    for name in ("node_cot", "coarse_cot", "edge_cot"):
        early.append(links.local(s[name], s["v_" + name]))
    pl.semaphore_wait(barrier, G - 1 + 24)

    lo, hi = pl.ds(0, N // 2), pl.ds(N // 2, N // 2)
    lat = s.node_lat
    a_lo = links.send(lat.at[lo], nodes.at[y, lo], links.at(y=y1))
    b_hi = links.send(lat.at[hi], nodes.at[y, hi], links.at(y=y3))
    a_hi = links.send(lat.at[hi], nodes.at[y, hi], links.at(y=y1))
    b_lo = links.send(lat.at[lo], nodes.at[y, lo], links.at(y=y3))

    lanes = lax.broadcasted_iota(jnp.int32, (E, 128), 1)
    subs = lax.broadcasted_iota(jnp.int32, (128, E), 0)

    def hot(code_row, hot_ref, hot_t_ref, width):
        across = jnp.broadcast_to(code_row, (128, E))
        down = jnp.transpose(across)
        for j in range(width // 128):
            hot_ref[:, j * 128 : (j + 1) * 128] = jnp.where(down == lanes + j * 128, 1.0, 0.0).astype(BF16)
            hot_t_ref[j * 128 : (j + 1) * 128, :] = jnp.where(across == subs + j * 128, 1.0, 0.0).astype(BF16)

    for copy in codes_copies + gain_copies:
        copy.wait()
    codes = s.v_halo_rows[...]
    spread = (
        lax.broadcasted_iota(jnp.int32, (G, G * HALO), 0)
        == lax.broadcasted_iota(jnp.int32, (G, G * HALO), 1) // HALO
    )
    spread = jnp.where(spread, 1.0, 0.0).astype(BF16)
    high = dot((codes // 16).astype(F32).astype(BF16), spread)
    low = dot((codes % 16).astype(F32).astype(BF16), spread)
    shape = (HALO, G * HALO)
    at_k = lax.broadcasted_iota(jnp.int32, shape, 0) == lax.broadcasted_iota(jnp.int32, shape, 1) % HALO
    codes = jnp.sum(jnp.where(at_k, high * 16.0 + low, 0.0), axis=0, keepdims=True).astype(jnp.int32)
    hot(codes, s.halo_hot, s.halo_hot_t, NY * N)
    for copy in early:
        copy.wait()

    a_lo.wait_recv()
    a2 = links.send(nodes.at[y1, lo], nodes.at[y1, lo], links.at(y=y3))
    b_hi.wait_recv()
    b2 = links.send(nodes.at[y3, hi], nodes.at[y3, hi], links.at(y=y1))

    def weight_rows(name, owner, first, count):
        rows = weights[name]
        return s[name].at[pl.ds(aligned(owner * rows + c * (rows // 2) + first, 16), count)]

    def weight_step1(group):
        copies = []
        for name in group:
            half = weights[name] // 2
            src = s["w_" + name].at[pl.ds(aligned(c * half, 16), half)]
            copies.append(
                (
                    name,
                    links.send(src, weight_rows(name, y, 0, half), links.at(y=y1)),
                    links.send(src, weight_rows(name, y, 0, half), links.at(y=y3)),
                )
            )
        return copies

    def weight_step2(copies):
        forward, swap = [], []
        for name, first, second in copies:
            half, quarter = weights[name] // 2, weights[name] // 4
            first.wait_recv()
            src = weight_rows(name, y1, 0, quarter)
            forward.append(links.send(src, src, links.at(y=y3)))
            src = weight_rows(name, y1, 0, half)
            swap.append(links.send(src, src, other))
            second.wait_recv()
            src = weight_rows(name, y3, quarter, quarter)
            forward.append(links.send(src, src, links.at(y=y1)))
            src = weight_rows(name, y3, 0, half)
            swap.append(links.send(src, src, other))
        return forward, swap

    def weight_step3(group, forward, swap):
        for copy in forward:
            copy.wait_recv()
        for name in group:
            src = weight_rows(name, y2, 0, weights[name] // 2)
            swap.append(links.send(src, src, other))
        return swap

    for copy in (a_hi, b_lo, a2, b2):
        copy.wait_recv()
    edge_weights = weight_step1(("ef", "es"))

    out_slots, in_slots = s.out_slots, s.in_slots
    part_nodes = nodes[...].reshape(NY * N, D)
    out_slots[...] = to_slots(dot(s.halo_hot[...], part_nodes))

    def graph_peer(j):
        to = (g + j * 29) % G
        return to, (to, y)

    halo_wait = links.send_many(
        G, graph_peer, lambda m: out_slots.at[m], in_slots.at[g], in_slots.at[pl.ds(0, G - 1)]
    )
    in_slots[g] = out_slots[g]

    live_copy.wait()
    live = s.live[0]
    alive_row = lax.broadcasted_iota(jnp.int32, (1, E), 1) < live
    hot(jnp.where(alive_row, s.v_senders[...], -1), s.send_hot, s.send_hot_t, 1280)
    hot(jnp.where(alive_row, s.v_receivers[...], -1), s.recv_hot, s.recv_hot_t, N + C)
    node_lat, coarse_lat = node_in[:N, :D], node_in[N:, :D]
    edge_in[:, 2 * D :] = (
        dot(s.recv_hot[:, :N], node_lat) + dot(s.recv_hot[:, N:], coarse_lat)
    ).astype(BF16)
    edge_in[:, D : 2 * D] = (
        dot(s.send_hot[:, :512], part_nodes) + dot(s.send_hot[:, 1024:], coarse_lat)
    ).astype(BF16)
    edge_forward, edge_swap = weight_step2(edge_weights)
    node_weights = weight_step1(("nf", "ns"))
    edge_swap = weight_step3(("ef", "es"), edge_forward, edge_swap)
    for copy in edge_swap:
        copy.wait_recv()
    before = s.before
    before[...] = dot(edge_in[:, :D], ef[:D]) + dot(edge_in[:, 2 * D :], ef[2 * D :])


    halo_wait()
    s.halo[...] = from_slots(in_slots[...])
    edge_in[:, D : 2 * D] = (
        edge_in[:, D : 2 * D].astype(F32) + dot(s.send_hot[:, 512:1024], s.halo[...])
    ).astype(BF16)
    before[...] = before[...] + dot(edge_in[:, D : 2 * D], ef[D : 2 * D])
    node_forward, node_swap = weight_step2(node_weights)
    s.hidden[...] = (before[...] * jax.nn.sigmoid(before[...])).astype(BF16)
    normed, inverse = normalise(dot(s.hidden[...], es[...]))
    s.normed[...] = normed
    s.inverse[...] = inverse
    edge_next = (edge_in[:, :D].astype(F32) + normed * s.v_edge_gain[...]).astype(BF16)
    s.coarse_part[...] = dot(s.recv_hot_t[N:], edge_next)
    total = coarse_sum(
        links, s.coarse_part, s.a1_src, s.a1_rs, s.a1_z, s.a1_ag, s.coarse_total
    )
    next(total)
    own_agg = dot(s.recv_hot_t[:N], edge_next).astype(BF16)
    node_in[:N, D:] = own_agg
    node_swap = weight_step3(("nf", "ns"), node_forward, node_swap)

    def node_up(rows):
        name = "v_node_cot" if rows.start == 0 else "v_coarse_cot"
        return s[name][...].astype(F32)

    def node_pass_forward(rows):
        a = dot(node_in[rows], nf[...])
        hidden = (a * jax.nn.sigmoid(a)).astype(BF16)
        s.n_before[rows] = a
        s.n_hidden[rows] = hidden
        n, inv = normalise(dot(hidden, ns[...]))
        s.n_normed[rows] = n
        s.n_inverse[rows] = inv

    def node_pass_backward(rows):
        up = node_up(rows)
        q = norm_backward(up, s.v_node_gain[...], s.n_normed[rows], s.n_inverse[rows])
        zz = silu_backward(dot_nt(q, ns[...]), s.n_before[rows])
        s.n_lin[rows] = q
        s.n_gbefore[rows] = zz
        s.gagg[rows] = dot_nt(zz, nf[D:]).astype(BF16)

    own, coarse = slice(0, N), slice(N, N + C)

    def fill_node(j, to):
        w = node_refs.w
        w[j, :256] = dot_tn(node_in[:N, pl.ds(aligned(to * 256, 128), 256)], s.n_gbefore[:N]).astype(BF16)
        w[j, 256:] = dot_tn(s.n_hidden[:N, pl.ds(aligned(to * 128, 128), 128)], s.n_lin[:N]).astype(BF16)

    node_job = node_weights_sum(links, node_refs, RN, fill_node, s.n_grad)
    next(total)
    for copy in node_swap:
        copy.wait_recv()
    node_pass_forward(own)
    node_pass_backward(own)
    next(node_job)
    next(total)
    next(node_job)
    s.edge_in_t[...] = jnp.transpose(edge_in[...])
    s.hidden_t[...] = jnp.transpose(s.hidden[...])
    for _ in total:
        pass
    node_in[N:, D:] = s.coarse_total[...]
    node_pass_forward(coarse)
    node_pass_backward(coarse)

    s.gnext[...] = s.v_edge_cot[...].astype(F32) + dot(s.recv_hot[...], s.gagg[...])
    alive = lax.broadcasted_iota(jnp.int32, (E, 1), 0) < live
    upstream = jnp.where(alive, s.gnext[...], 0.0)
    q = norm_backward(upstream, s.v_edge_gain[...], s.normed[...], s.inverse[...])
    s.lin[...] = q
    s.gbefore[...] = silu_backward(dot_nt(q, es[...]), before[...])
    gbefore = s.gbefore

    next(node_job)

    def fill_ea(j, to):
        ea_refs.w[j] = dot(s.edge_in_t[pl.ds(aligned(to * 384, 128), 256), :], gbefore[...]).astype(BF16)

    def fill_eb(j, to):
        first = dot(s.edge_in_t[pl.ds(aligned(to * 384 + 256, 128), 128), :], gbefore[...])
        second = dot(s.hidden_t[pl.ds(aligned(to * 128, 128), 128), :], s.lin[...])
        eb_refs.w[j, :128] = first.astype(BF16)
        eb_refs.w[j, 128:] = second.astype(BF16)

    ea_job = edge_weights_sum(links, ea_refs, RE, fill_ea, s.ea_grad)
    eb_job = edge_weights_sum(links, eb_refs, RE, fill_eb, s.eb_grad)
    next(ea_job)
    next(eb_job)
    moved = s.moved
    moved[...] = dot_nt(gbefore[...], ef[D : 2 * D]).astype(BF16)
    back_out, back_in = s.back_out, s.back_in
    back_out[...] = to_slots(dot(s.send_hot_t[512:1024], moved[...]))
    back_wait = links.send_many(
        G, graph_peer, lambda m: back_out.at[m], back_in.at[g], back_in.at[pl.ds(0, G - 1)]
    )
    back_in[g] = back_out[g]
    next(ea_job)
    next(eb_job)
    next(node_job)
    s.part_grads[...] = dot(s.send_hot_t[:512], moved[...])
    s.coarse_part[...] = dot(s.send_hot_t[1024:], moved[...])
    moved[...] = dot_nt(gbefore[...], ef[2 * D :]).astype(BF16)
    s.coarse_part[...] = s.coarse_part[...] + dot(s.recv_hot_t[N:], moved[...])
    s.recv_own[...] = dot(s.recv_hot_t[:N], moved[...])
    s.edge_grad[...] = s.gnext[...] + dot_nt(gbefore[...], ef[:D])
    s.direct[:N] = s.v_node_cot[...].astype(F32) + dot_nt(s.n_gbefore[:N], nf[:D])
    s.direct[N:] = s.v_coarse_cot[...].astype(F32) + dot_nt(s.n_gbefore[N:], nf[:D])
    extra = node_refs.extra
    first = dot_tn(node_in[N:, pl.ds(aligned(y * 256, 128), 256)], s.n_gbefore[N:])
    extra[0, :RN] = first[:RN]
    extra[1, : 256 - RN] = first[RN:]
    extra[1, 256 - RN : RN] = dot_tn(s.n_hidden[N:, pl.ds(aligned(y * 128, 128), 128)], s.n_lin[N:])
    extra[:, RN:] = jnp.zeros((NC, NZ * ZR - RN, D), F32)
    next(ea_job)
    next(node_job)
    next(eb_job)
    coarse_grad = s.coarse_grad
    total = coarse_sum(links, s.coarse_part, s.a2_src, s.a2_rs, s.a2_z, s.a2_ag, coarse_grad)
    next(total)
    next(ea_job)
    next(eb_job)

    back_wait()
    s.halo[...] = from_slots(back_in[...])
    s.part_grads[...] = s.part_grads[...] + dot(s.halo_hot_t[...], s.halo[...])
    p_y = s.p_y
    for j in range(4):
        p_y[j] = s.part_grads[pl.ds(aligned(xor4(y, j) * N, 16), N), :].astype(BF16)
    node_grad = s.node_grad
    part_job = halving(
        links, p_y, N // 2, s.p_a1, s.p_b1, s.p_a2, s.p_b2, lambda j: links.at(y=xor4(y, j)), node_grad
    )
    next(part_job)
    next(total)
    next(node_job)
    next(ea_job)
    next(total)
    next(part_job)
    next(node_job)
    next(eb_job)
    for _ in part_job:
        pass
    node_grad[...] = node_grad[...] + s.direct[:N] + s.recv_own[...]
    for _ in total:
        pass
    coarse_grad[...] = coarse_grad[...] + s.direct[N:]
    next(ea_job)
    next(node_job)
    next(eb_job)
    for job in (ea_job, node_job, eb_job):
        for _ in job:
            pass
    links.finish()


def finish(*refs):
    sources, results, held, sems = refs[:6], refs[6:13], refs[13:17], refs[17]
    ea_grad, eb_grad, n_grad = sources[3:]
    ef, es, nf, ns = held
    stores = [
        pltpu.make_async_copy(src, dst, sems.at[k])
        for k, (src, dst) in enumerate(zip((*sources[:3], *held), results))
    ]
    for k in range(3):
        stores[k].start()
    for i in range(4 * RE // 16):
        row = i * 16
        pieces, core, block = (ea_grad, eb_grad)[i // 16], (i // 8) % 2, i % 8
        out, at = (ef, row) if row < 384 else (es, row - 384)
        for j in range(4):
            out[at : at + 16, j * 128 : (j + 1) * 128] = pieces[core, 4 * block + j].astype(F32)
    stores[3].start()
    stores[4].start()
    for i in range(2 * RN // ZR):
        row = i * ZR
        out, at = (nf, row) if row < 256 else (ns, row - 256)
        for j in range(NX):
            out[at : at + ZR, j * 128 : (j + 1) * 128] = n_grad[row // RN, j, (row % RN) // ZR].astype(F32)
    stores[5].start()
    stores[6].start()
    for copy in stores:
        copy.wait()


def program(
    node_lat, coarse_lat, edge_lat, senders, receivers, halo_rows, edge_live, edge_first, edge_second,
    node_first, node_second, edge_gain, node_gain, node_cotangent, coarse_cotangent, edge_cotangent,
):
    vmem, anywhere = pl.BlockSpec(memory_space=pltpu.VMEM), pl.BlockSpec(memory_space=pl.ANY)
    semaphores = [pltpu.SemaphoreType.DMA((count,)) for count in (SENDS, SENDS, LOCALS)]
    results = pl.pallas_call(
        body,
        out_shape=[pltpu.VMEM(*v) for v in OUTPUTS.values()],
        in_specs=[anywhere] * len(INPUTS),
        out_specs=[vmem] * len(OUTPUTS),
        scratch_shapes=[pltpu.VMEM(*v) for d in (SCRATCH, EDGE_JOB, EDGE_JOB, NODE_JOB) for v in d.values()]
        + [pltpu.SMEM((1,), jnp.int32)] + semaphores,
        compiler_params=pltpu.CompilerParams(
            collective_id=0, has_side_effects=True, vmem_limit_bytes=60 * 1024 * 1024
        ),
        name="layer",
    )(
        node_lat,
        coarse_lat,
        edge_lat,
        senders.reshape(1, E),
        receivers.reshape(1, E),
        halo_rows.T,
        edge_live,
        edge_first,
        edge_second,
        node_first,
        node_second,
        edge_gain.reshape(1, D),
        node_gain.reshape(1, D),
        node_cotangent,
        coarse_cotangent,
        edge_cotangent,
    )
    shapes = [(N, D), (C, D), (E, D), (384, D), (128, D), (256, D), (128, D)]
    return pl.pallas_call(
        finish,
        out_shape=[jax.ShapeDtypeStruct(v, F32) for v in shapes],
        in_specs=[vmem] * 6,
        out_specs=[anywhere] * 7,
        scratch_shapes=[pltpu.VMEM(v, F32) for v in shapes[3:]] + [pltpu.SemaphoreType.DMA((7,))],
        compiler_params=pltpu.CompilerParams(vmem_limit_bytes=60 * 1024 * 1024),
        name="finish",
    )(*(pltpu.with_memory_space_constraint(v, pltpu.VMEM) for v in results))


def solution(mesh):
    rows = P(("graph", "feat"), None)
    return jax.shard_map(
        program,
        mesh=mesh,
        in_specs=(
            rows, P(), rows, P(("graph", "feat")), P(("graph", "feat")), rows, P(("graph", "feat")),
            P("feat", None), P("feat", None), P("feat", None), P("feat", None), P(), P(), rows, P(), rows,
        ),
        out_specs=(
            rows, P(), rows, P("feat", None), P("feat", None), P("feat", None), P("feat", None),
        ),
        check_vma=False,
    )
```

```python
import functools

import jax
import jax.numpy as jnp
from jax import lax
from jax.experimental import pallas as pl
from jax.experimental.pallas import tpu as pltpu
from jax.sharding import PartitionSpec as P

NORM_EPSILON = 1e-05
F32 = jnp.float32
BF16 = jnp.bfloat16
MESH = pl.DeviceIdType.MESH

D = 512
N = 128
E = 512
C = 256
NX, NY, NZ, NC = 4, 4, 8, 2
G = NX * NZ * NC
HALO = 8
RE, RN = 128, 192
ZR = 32
PLANE = NX * NZ


def dot(a, b):
    return jnp.dot(a, b, preferred_element_type=F32)


def dot_nt(a, b):
    return lax.dot_general(a, b, (((1,), (1,)), ((), ())), preferred_element_type=F32)


def dot_tn(a, b):
    return lax.dot_general(a, b, (((0,), (0,)), ((), ())), preferred_element_type=F32)


def xor4(v, j):
    return (v, v + 1 - 2 * (v % 2), (v + 2) % 4, 3 - v)[j]


def aligned(index, by):
    return pl.multiple_of(index, by)


def normalise(output):
    centred = output - jnp.mean(output, axis=1, keepdims=True)
    inverse = lax.rsqrt(jnp.mean(centred * centred, axis=1, keepdims=True) + NORM_EPSILON)
    return centred * inverse, inverse


def norm_backward(upstream, gain, normed, inverse):
    scaled = upstream * gain
    grad = inverse * (
        scaled
        - jnp.mean(scaled, axis=1, keepdims=True)
        - normed * jnp.mean(scaled * normed, axis=1, keepdims=True)
    )
    return grad.astype(BF16)


def silu_slope(before):
    sigma = jax.nn.sigmoid(before)
    return sigma * (1.0 + before * (1.0 - sigma))


SCRATCH = dict(
    nodes=((NY, N, D), BF16),
    ef=((3 * D, D), BF16),
    es=((D, D), BF16),
    nf=((2 * D, D), BF16),
    ns=((D, D), BF16),
    halo_hot=((G * HALO, NY * N), BF16),
    halo_hot_t=((NY * N, G * HALO), BF16),
    send_hot=((E, 1280), BF16),
    send_hot_t=((1280, E), BF16),
    recv_hot=((E, N + C), BF16),
    recv_hot_t=((N + C, E), BF16),
    out_slots=((G, 16, 256), BF16),
    in_slots=((G, 16, 256), BF16),
    back_out=((G, 16, 256), BF16),
    back_in=((G, 16, 256), BF16),
    halo=((G * HALO, D), BF16),
    edge_in=((E, 3 * D), BF16),
    edge_in_t=((3 * D, E), BF16),
    hidden_t=((D, E), BF16),
    before=((E, D), F32),
    hidden=((E, D), BF16),
    normed=((E, D), F32),
    inverse=((E, 1), F32),
    lin=((E, D), BF16),
    gbefore=((E, D), BF16),
    gnext=((E, D), F32),
    moved=((E, D), BF16),
    node_in=((N + C, 2 * D), BF16),
    n_before=((N + C, D), F32),
    n_hidden=((N + C, D), BF16),
    n_normed=((N + C, D), F32),
    n_inverse=((N + C, 1), F32),
    n_lin=((N + C, D), BF16),
    n_gbefore=((N + C, D), BF16),
    direct=((N + C, D), F32),
    gagg=((N + C, D), BF16),
    coarse_total=((C, D), BF16),
    coarse_part=((C, D), F32),
    recv_own=((N, D), F32),
    part_grads=((NY * N, D), F32),
    a1_src=((32, 16, 256), BF16),
    a1_rs=((32, 16, 256), BF16),
    a1_z=((NZ, 16, 256), BF16),
    a1_ag=((32, 16, 256), BF16),
    a2_out=((C // 2, D), BF16),
    a2_in=((C // 2, D), BF16),
    a2_src=((16, 16, 256), BF16),
    a2_rs=((16, 16, 256), BF16),
    a2_z=((NZ, 16, 256), BF16),
    a2_ag=((16, 16, 256), BF16),
    a2_back=((16, 16, 256), BF16),
    coarse_base=((C, D), F32),
    slope=((E, D), F32),
    v_halo_rows=((HALO, G), jnp.int32),
    v_senders=((1, E), jnp.int32),
    v_receivers=((1, E), jnp.int32),
    v_edge_gain=((1, D), F32),
    v_node_gain=((1, D), F32),
    v_node_cot=((N, D), BF16),
    v_coarse_cot=((C, D), BF16),
    v_edge_cot=((E, D), BF16),
    p_y=((NY, N, D), BF16),
    p_a1=((2, N // 2, D), BF16),
    p_b1=((2, N // 2, D), BF16),
    p_a2=((N // 2, D), BF16),
    p_b2=((N // 2, D), BF16),
)


def job_scratch(r):
    return dict(
        w=((NY, 2 * r, D), BF16),
        c=((NY, r, D), BF16),
        y=((NY, r, D), BF16),
        ya1=((2, r // 2, D), BF16),
        yb1=((2, r // 2, D), BF16),
        ya2=((r // 2, D), BF16),
        yb2=((r // 2, D), BF16),
        sum=((r, D), F32),
    )


EDGE_JOB, NODE_JOB = job_scratch(RE), job_scratch(RN)
EDGE_JOB.update(
    x=((NX, RE, 128), BF16),
    xr=((NX, RE, 128), BF16),
    zs=((NZ, 16, 128), BF16),
    zr=((NZ, 16, 128), BF16),
    g=((PLANE, 16, 128), BF16),
)
NODE_JOB.update(
    x=((NX, RN, 128), BF16),
    xr=((NX, RN, 128), BF16),
    zs=((NZ, ZR, 128), BF16),
    zr=((NZ, ZR, 128), BF16),
    g=((NX, NZ, ZR, 128), BF16),
    extra=((NC, NZ * ZR, D), F32),
)
SENDS, LOCALS = 85, 17

INPUTS = (
    "node_lat", "coarse_lat", "edge_lat", "senders", "receivers", "halo_rows", "edge_live", "w_ef", "w_es",
    "w_nf", "w_ns", "edge_gain", "node_gain", "node_cot", "coarse_cot", "edge_cot",
)
OUTPUTS = dict(
    node_grad=((N, D), F32),
    coarse_grad=((C, D), F32),
    edge_grad=((E, D), F32),
    ea_grad=((NC, PLANE, 16, 128), BF16),
    eb_grad=((NC, PLANE, 16, 128), BF16),
    n_grad=((NC, NX, NZ, ZR, 128), BF16),
)


class Refs(dict):
    __getattr__ = dict.__getitem__


class Links:
    def __init__(self, send_sems, recv_sems, local_sems):
        self.send_sems, self.recv_sems, self.used, self.sent = send_sems, recv_sems, 0, []
        self.local_sems, self.local_used = local_sems, 0
        graph = lax.axis_index("graph")
        self.g, self.y = graph, lax.axis_index("feat")
        self.c, self.z, self.x = graph % 2, (graph // 2) % 8, graph // 16

    def slot(self):
        self.used += 1
        return self.used - 1

    def at(self, x=None, y=None, z=None, c=None):
        x = self.x if x is None else x
        y = self.y if y is None else y
        z = self.z if z is None else z
        c = self.c if c is None else c
        return ((x * 8 + z) * 2 + c, y)

    def local(self, src, dst):
        copy = pltpu.make_async_copy(src, dst, self.local_sems.at[self.local_used])
        self.local_used += 1
        copy.start()
        return copy

    def send(self, src, dst, device):
        k = self.slot()
        copy = pltpu.make_async_remote_copy(
            src_ref=src,
            dst_ref=dst,
            send_sem=self.send_sems.at[k],
            recv_sem=self.recv_sems.at[k],
            device_id=device,
            device_id_type=MESH,
        )
        copy.start()
        self.sent.append(copy)
        return copy

    def send_many(self, count, peer, src, dst, whole):
        k = self.slot()

        for j in range(1, count):
            index, device = peer(j)
            pltpu.make_async_remote_copy(
                src_ref=src(index),
                dst_ref=dst,
                send_sem=self.send_sems.at[k],
                recv_sem=self.recv_sems.at[k],
                device_id=device,
                device_id_type=MESH,
            ).start()
        self.sent.append(("many", whole, k))

        def wait():
            pltpu.make_async_copy(whole, whole, self.recv_sems.at[k]).wait()

        return wait

    def finish(self):
        for copy in self.sent:
            if isinstance(copy, tuple):
                pltpu.make_async_copy(copy[1], copy[1], self.send_sems.at[copy[2]]).wait()
            else:
                copy.wait_send()


def to_slots(rows):
    rows = rows.reshape(G, HALO, D)
    return jnp.concatenate([rows[:, :, :256], rows[:, :, 256:]], axis=1).astype(BF16)


def from_slots(slots):
    slots = slots.astype(F32)
    rows = jnp.concatenate([slots[:, :8, :], slots[:, 8:, :]], axis=2)
    return rows.reshape(G * HALO, D).astype(BF16)


def halving(links, buf, half, ra1, rb1, ra2, rb2, partner, total_out):
    lo, hi = pl.ds(0, half), pl.ds(half, half)
    p1, p3 = partner(1), partner(3)
    a = links.send(buf.at[pl.ds(1, 2), lo], ra1, p1)
    b = links.send(buf.at[pl.ds(2, 2), hi], rb1, p3)
    yield
    a.wait_recv()
    buf[3, lo] = (buf[3, lo].astype(F32) + ra1[1].astype(F32)).astype(BF16)
    a = links.send(buf.at[3, lo], ra2, p3)
    b.wait_recv()
    buf[1, hi] = (buf[1, hi].astype(F32) + rb1[0].astype(F32)).astype(BF16)
    b = links.send(buf.at[1, hi], rb2, p1)
    total_out[lo] = buf[0, lo].astype(F32) + ra1[0].astype(F32)
    total_out[hi] = buf[0, hi].astype(F32) + rb1[1].astype(F32)
    yield
    a.wait_recv()
    total_out[lo] = total_out[lo] + ra2[...].astype(F32)
    b.wait_recv()
    total_out[hi] = total_out[hi] + rb2[...].astype(F32)


def coarse_sum(links, source, src, rs, zb, ag, out):
    me = (links.x * 4 + links.y) * 2 + links.c

    def peer(j):
        dx, dy, dc = (j * 11 % 32) // 8, (j * 11 % 8) // 2, j % 2
        px, py, pc = lax.rem(links.x + dx, NX), lax.rem(links.y + dy, NY), 1 - links.c if dc else links.c
        return (px * 4 + py) * 2 + pc, links.at(x=px, y=py, c=pc)

    for i in range(32):
        src[i] = source[(i // 2) * 16 : (i // 2) * 16 + 16, (i % 2) * 256 : (i % 2) * 256 + 256].astype(BF16)
    wait = links.send_many(32, peer, lambda m: src.at[m], rs.at[me], rs.at[pl.ds(0, 31)])
    rs[me] = src[me]
    yield
    wait()
    zb[links.z] = jnp.sum(rs[...].astype(F32), axis=0).astype(BF16)

    def along(j):
        to = lax.rem(links.z + j * 3 % NZ, NZ)
        return to, links.at(z=to)

    wait = links.send_many(8, along, lambda m: zb.at[links.z], zb.at[links.z], zb.at[pl.ds(0, 7)])
    yield
    wait()
    ag[me] = jnp.sum(zb[...].astype(F32), axis=0).astype(BF16)
    wait = links.send_many(32, peer, lambda m: ag.at[me], ag.at[me], ag.at[pl.ds(0, 31)])
    yield
    wait()
    for i in range(32):
        out[(i // 2) * 16 : (i // 2) * 16 + 16, (i % 2) * 256 : (i % 2) * 256 + 256] = ag[i].astype(out.dtype)


def coarse_sum_by_chip(links, s, out):
    half = C // 2
    mine, theirs = aligned(links.c * half, 16), aligned((1 - links.c) * half, 16)
    other = links.at(c=1 - links.c)
    s.a2_out[...] = s.coarse_part[pl.ds(theirs, half), :].astype(BF16)
    copy = links.send(s.a2_out, s.a2_in, other)
    yield
    copy.wait_recv()
    source = s.coarse_part[pl.ds(mine, half), :] + s.a2_in[...].astype(F32)
    me = links.x * NY + links.y

    def peer(j):
        px, py = lax.rem(links.x + (j * 7 % 16) // 4, NX), lax.rem(links.y + j * 7 % 4, NY)
        return px * NY + py, links.at(x=px, y=py)

    for i in range(16):
        s.a2_src[i] = source[(i // 2) * 16 : (i // 2) * 16 + 16, (i % 2) * 256 : (i % 2) * 256 + 256].astype(BF16)
    wait = links.send_many(16, peer, lambda m: s.a2_src.at[m], s.a2_rs.at[me], s.a2_rs.at[pl.ds(0, 15)])
    s.a2_rs[me] = s.a2_src[me]
    yield
    wait()
    zb = s.a2_z
    zb[links.z] = jnp.sum(s.a2_rs[...].astype(F32), axis=0).astype(BF16)

    def along(j):
        to = lax.rem(links.z + j * 3 % NZ, NZ)
        return to, links.at(z=to)

    wait = links.send_many(NZ, along, lambda m: zb.at[links.z], zb.at[links.z], zb.at[pl.ds(0, NZ - 1)])
    yield
    wait()
    ag = s.a2_ag
    ag[me] = jnp.sum(zb[...].astype(F32), axis=0).astype(BF16)
    wait = links.send_many(16, peer, lambda m: ag.at[me], ag.at[me], ag.at[pl.ds(0, 15)])
    yield
    wait()
    copy = links.send(ag, s.a2_back, other)
    for i in range(16):
        rows = pl.ds(aligned(mine + (i // 2) * 16, 16), 16)
        out[rows, (i % 2) * 256 : (i % 2) * 256 + 256] = ag[i].astype(out.dtype)
    yield
    copy.wait_recv()
    for i in range(16):
        rows = pl.ds(aligned(theirs + (i // 2) * 16, 16), 16)
        out[rows, (i % 2) * 256 : (i % 2) * 256 + 256] = s.a2_back[i].astype(out.dtype)


def weight_scatter(links, t, r, fill):
    w, cin, ybuf = t.w, t.c, t.y
    other = links.at(c=1 - links.c)
    theirs = pl.ds(aligned((1 - links.c) * r, 16), r)
    mine = pl.ds(aligned(links.c * r, 16), r)
    copies = {}
    for j in (2, 1, 3, 0):
        fill(j, xor4(links.y, j))
        copies[j] = links.send(w.at[j, theirs], cin.at[j], other)
    yield
    for j in (2, 1, 3, 0):
        copies[j].wait_recv()
        ybuf[j] = (w[j, mine].astype(F32) + cin[j].astype(F32)).astype(BF16)
    total = t.sum
    yield from halving(
        links, ybuf, r // 2, t.ya1, t.yb1, t.ya2, t.yb2,
        lambda j: links.at(y=xor4(links.y, j)), total,
    )


def edge_weights_sum(links, t, r, fill, out):
    yield from weight_scatter(links, t, r, fill)
    for j in range(NX):
        t.x[j] = t.sum[:, j * 128 : (j + 1) * 128].astype(BF16)

    def across(j):
        to = lax.rem(links.x + j, NX)
        return to, links.at(x=to)

    def along(j):
        to = lax.rem(links.z + j * 3 % NZ, NZ)
        return to, links.at(z=to)

    wait = links.send_many(NX, across, lambda m: t.x.at[m], t.xr.at[links.x], t.xr.at[pl.ds(0, NX - 1)])
    t.xr[links.x] = t.x[links.x]
    yield
    wait()
    t.zs[...] = jnp.sum(t.xr[...].astype(F32), axis=0).astype(BF16).reshape(NZ, 16, 128)
    wait = links.send_many(NZ, along, lambda m: t.zs.at[m], t.zr.at[links.z], t.zr.at[pl.ds(0, NZ - 1)])
    t.zr[links.z] = t.zs[links.z]
    yield
    wait()
    gathered = t.g
    me = links.x * NZ + links.z

    def peer(k):
        px, pz = lax.rem(links.x + (k * 11 % 32) // 8, NX), lax.rem(links.z + k * 11 % 8, NZ)
        return px * NZ + pz, links.at(x=px, z=pz)

    gathered[me] = jnp.sum(t.zr[...].astype(F32), axis=0).astype(BF16)
    wait = links.send_many(
        PLANE, peer, lambda m: gathered.at[me], gathered.at[me], gathered.at[pl.ds(0, PLANE - 1)]
    )
    yield
    wait()
    copy = links.send(gathered, out.at[links.c], links.at(c=1 - links.c))
    out[links.c] = gathered[...]
    yield
    copy.wait_recv()


def node_weights_sum(links, t, r, fill, out):
    yield from weight_scatter(links, t, r, fill)
    for j in range(NX):
        t.x[j] = t.sum[:, j * 128 : (j + 1) * 128].astype(BF16)

    def across(j):
        to = lax.rem(links.x + j, NX)
        return to, links.at(x=to)

    wait = links.send_many(NX, across, lambda m: t.x.at[m], t.xr.at[links.x], t.xr.at[pl.ds(0, NX - 1)])
    t.xr[links.x] = t.x[links.x]
    yield
    wait()
    sub = jnp.sum(t.xr[...].astype(F32), axis=0)
    blocks = r // ZR
    for i in range(NZ):
        t.zs[i] = sub[i * ZR : (i + 1) * ZR].astype(BF16) if i < blocks else jnp.zeros((ZR, 128), BF16)

    def along(j):
        to = lax.rem(links.z + j * 3 % NZ, NZ)
        return to, links.at(z=to)

    wait = links.send_many(NZ, along, lambda m: t.zs.at[m], t.zr.at[links.z], t.zr.at[pl.ds(0, NZ - 1)])
    t.zr[links.z] = t.zs[links.z]
    yield
    wait()
    own = t.g.at[links.x]
    extra = t.extra[
        links.c, pl.ds(aligned(links.z * ZR, ZR), ZR), pl.ds(aligned(links.x * 128, 128), 128)
    ]
    own[links.z] = (jnp.sum(t.zr[...].astype(F32), axis=0) + extra).astype(BF16)
    wait = links.send_many(NZ, along, lambda m: own.at[links.z], own.at[links.z], own.at[pl.ds(0, NZ - 1)])
    yield
    wait()
    every = pl.ds(0, blocks)
    mine = t.g.at[links.x, every]
    wait = links.send_many(NX, across, lambda m: mine, mine, t.g.at[pl.ds(0, NX - 1), every])
    yield
    wait()
    result = t.g.at[:, every]
    copy = links.send(result, out.at[links.c, :, every], links.at(c=1 - links.c))
    out[links.c] = t.g[...]
    yield
    copy.wait_recv()


def body(*refs):
    refs = iter(refs)
    s = Refs(zip([*INPUTS, *OUTPUTS, *SCRATCH], refs))
    ea_refs, eb_refs = Refs(zip(EDGE_JOB, refs)), Refs(zip(EDGE_JOB, refs))
    node_refs = Refs(zip(NODE_JOB, refs))
    s.update(live=next(refs))
    links = Links(*refs)
    x, y, z, c, g = links.x, links.y, links.z, links.c, links.g
    y1, y2, y3 = xor4(y, 1), xor4(y, 2), xor4(y, 3)
    other = links.at(c=1 - c)
    ef, es, nf, ns = s.ef, s.es, s.nf, s.ns
    weights = {"ef": 384, "es": 128, "nf": 256, "ns": 128}
    nodes, edge_in, node_in = s.nodes, s.edge_in, s.node_in

    barrier = pltpu.get_barrier_semaphore()

    for j in range(1, G):
        pl.semaphore_signal(barrier, inc=1, device_id=((g + j) % G, y), device_id_type=MESH)
    for k in range(NX * NC):
        for there in (y1, y2, y3):
            pl.semaphore_signal(
                barrier, inc=1, device_id=links.at(x=k // 2, c=k % 2, y=there), device_id_type=MESH
            )
    live_copy = links.local(s.edge_live, s.live)
    codes_copies = [links.local(s[name], s["v_" + name]) for name in ("halo_rows", "senders", "receivers")]
    gain_copies = [links.local(s[name], s["v_" + name]) for name in ("edge_gain", "node_gain")]
    early = [
        links.local(s.node_lat, nodes.at[y]),
        links.local(s.node_lat, node_in.at[pl.ds(0, N), pl.ds(0, D)]),
        links.local(s.coarse_lat, node_in.at[pl.ds(N, C), pl.ds(0, D)]),
        links.local(s.edge_lat, edge_in.at[:, pl.ds(0, D)]),
    ]
    for name, rows in weights.items():
        early.append(links.local(s["w_" + name], s[name].at[pl.ds(aligned(y * rows, 16), rows)]))
    for name in ("node_cot", "coarse_cot", "edge_cot"):
        early.append(links.local(s[name], s["v_" + name]))
    pl.semaphore_wait(barrier, G - 1 + 24)

    lo, hi = pl.ds(0, N // 2), pl.ds(N // 2, N // 2)
    lat = s.node_lat
    a_lo = links.send(lat.at[lo], nodes.at[y, lo], links.at(y=y1))
    b_hi = links.send(lat.at[hi], nodes.at[y, hi], links.at(y=y3))
    a_hi = links.send(lat.at[hi], nodes.at[y, hi], links.at(y=y1))
    b_lo = links.send(lat.at[lo], nodes.at[y, lo], links.at(y=y3))

    lanes = lax.broadcasted_iota(jnp.int32, (E, 128), 1)
    subs = lax.broadcasted_iota(jnp.int32, (128, E), 0)

    def hot(code_row, hot_ref, hot_t_ref, width):
        across = jnp.broadcast_to(code_row, (128, E))
        down = jnp.transpose(across)
        for j in range(width // 128):
            hot_ref[:, j * 128 : (j + 1) * 128] = jnp.where(down == lanes + j * 128, 1.0, 0.0).astype(BF16)
            hot_t_ref[j * 128 : (j + 1) * 128, :] = jnp.where(across == subs + j * 128, 1.0, 0.0).astype(BF16)

    for copy in codes_copies + gain_copies:
        copy.wait()
    codes = s.v_halo_rows[...]
    spread = (
        lax.broadcasted_iota(jnp.int32, (G, G * HALO), 0)
        == lax.broadcasted_iota(jnp.int32, (G, G * HALO), 1) // HALO
    )
    spread = jnp.where(spread, 1.0, 0.0).astype(BF16)
    high = dot((codes // 16).astype(F32).astype(BF16), spread)
    low = dot((codes % 16).astype(F32).astype(BF16), spread)
    shape = (HALO, G * HALO)
    at_k = lax.broadcasted_iota(jnp.int32, shape, 0) == lax.broadcasted_iota(jnp.int32, shape, 1) % HALO
    codes = jnp.sum(jnp.where(at_k, high * 16.0 + low, 0.0), axis=0, keepdims=True).astype(jnp.int32)
    hot(codes, s.halo_hot, s.halo_hot_t, NY * N)
    for copy in early:
        copy.wait()

    a_lo.wait_recv()
    a2 = links.send(nodes.at[y1, lo], nodes.at[y1, lo], links.at(y=y3))
    b_hi.wait_recv()
    b2 = links.send(nodes.at[y3, hi], nodes.at[y3, hi], links.at(y=y1))

    def weight_rows(name, owner, first, count):
        rows = weights[name]
        return s[name].at[pl.ds(aligned(owner * rows + c * (rows // 2) + first, 16), count)]

    def weight_step1(group):
        copies = []
        for name in group:
            half = weights[name] // 2
            src = s["w_" + name].at[pl.ds(aligned(c * half, 16), half)]
            copies.append(
                (
                    name,
                    links.send(src, weight_rows(name, y, 0, half), links.at(y=y1)),
                    links.send(src, weight_rows(name, y, 0, half), links.at(y=y3)),
                )
            )
        return copies

    def weight_step2(copies):
        forward, swap = [], []
        for name, first, second in copies:
            half, quarter = weights[name] // 2, weights[name] // 4
            first.wait_recv()
            src = weight_rows(name, y1, 0, quarter)
            forward.append(links.send(src, src, links.at(y=y3)))
            src = weight_rows(name, y1, 0, half)
            swap.append(links.send(src, src, other))
            second.wait_recv()
            src = weight_rows(name, y3, quarter, quarter)
            forward.append(links.send(src, src, links.at(y=y1)))
            src = weight_rows(name, y3, 0, half)
            swap.append(links.send(src, src, other))
        return forward, swap

    def weight_step3(group, forward, swap):
        for copy in forward:
            copy.wait_recv()
        for name in group:
            src = weight_rows(name, y2, 0, weights[name] // 2)
            swap.append(links.send(src, src, other))
        return swap

    edge_weights = weight_step1(("ef", "es"))
    for copy in (a_hi, b_lo, a2, b2):
        copy.wait_recv()

    out_slots, in_slots = s.out_slots, s.in_slots
    part_nodes = nodes[...].reshape(NY * N, D)
    out_slots[...] = to_slots(dot(s.halo_hot[...], part_nodes))

    def graph_peer(j):
        q, odd, r = (j - 1) // 16, (j - 1) % 2, (((j - 1) % 16) // 2 + 1) % 8
        dx, dz, dc = r // 2, (4 - q + odd * (1 + 2 * q)) % NZ, r % 2
        to = (lax.rem(x + dx, NX) * NZ + lax.rem(z + dz, NZ)) * NC + (1 - c if dc else c)
        return to, (to, y)

    halo_wait = links.send_many(
        G, graph_peer, lambda m: out_slots.at[m], in_slots.at[g], in_slots.at[pl.ds(0, G - 1)]
    )
    in_slots[g] = out_slots[g]

    live_copy.wait()
    live = s.live[0]
    alive_row = lax.broadcasted_iota(jnp.int32, (1, E), 1) < live
    hot(jnp.where(alive_row, s.v_senders[...], -1), s.send_hot, s.send_hot_t, 1280)
    hot(jnp.where(alive_row, s.v_receivers[...], -1), s.recv_hot, s.recv_hot_t, N + C)
    node_lat, coarse_lat = node_in[:N, :D], node_in[N:, :D]
    edge_in[:, 2 * D :] = (
        dot(s.recv_hot[:, :N], node_lat) + dot(s.recv_hot[:, N:], coarse_lat)
    ).astype(BF16)
    edge_in[:, D : 2 * D] = (
        dot(s.send_hot[:, :512], part_nodes) + dot(s.send_hot[:, 1024:], coarse_lat)
    ).astype(BF16)
    edge_forward, edge_swap = weight_step2(edge_weights)
    node_weights = weight_step1(("nf", "ns"))
    edge_swap = weight_step3(("ef", "es"), edge_forward, edge_swap)
    for copy in edge_swap:
        copy.wait_recv()
    before = s.before
    before[...] = dot(edge_in[:, :D], ef[:D]) + dot(edge_in[:, 2 * D :], ef[2 * D :])


    halo_wait()
    s.halo[...] = from_slots(in_slots[...])
    edge_in[:, D : 2 * D] = (
        edge_in[:, D : 2 * D].astype(F32) + dot(s.send_hot[:, 512:1024], s.halo[...])
    ).astype(BF16)
    before[...] = before[...] + dot(edge_in[:, D : 2 * D], ef[D : 2 * D])
    node_forward, node_swap = weight_step2(node_weights)
    s.hidden[...] = (before[...] * jax.nn.sigmoid(before[...])).astype(BF16)
    normed, inverse = normalise(dot(s.hidden[...], es[...]))
    s.normed[...] = normed
    s.inverse[...] = inverse
    edge_next = (edge_in[:, :D].astype(F32) + normed * s.v_edge_gain[...]).astype(BF16)
    s.coarse_part[...] = dot(s.recv_hot_t[N:], edge_next)
    total = coarse_sum(
        links, s.coarse_part, s.a1_src, s.a1_rs, s.a1_z, s.a1_ag, s.coarse_total
    )
    next(total)
    own_agg = dot(s.recv_hot_t[:N], edge_next).astype(BF16)
    node_in[:N, D:] = own_agg
    node_swap = weight_step3(("nf", "ns"), node_forward, node_swap)

    def node_up(rows):
        name = "v_node_cot" if rows.start == 0 else "v_coarse_cot"
        return s[name][...].astype(F32)

    def node_pass_forward(rows):
        if rows.start == 0:
            a = dot(node_in[rows], nf[...])
        else:
            a = s.coarse_base[...] + dot(node_in[rows, D:], nf[D:])
        hidden = (a * jax.nn.sigmoid(a)).astype(BF16)
        s.n_before[rows] = a
        s.n_hidden[rows] = hidden
        n, inv = normalise(dot(hidden, ns[...]))
        s.n_normed[rows] = n
        s.n_inverse[rows] = inv

    def node_pass_backward(rows):
        up = node_up(rows)
        q = norm_backward(up, s.v_node_gain[...], s.n_normed[rows], s.n_inverse[rows])
        zz = (dot_nt(q, ns[...]) * silu_slope(s.n_before[rows])).astype(BF16)
        s.n_lin[rows] = q
        s.n_gbefore[rows] = zz
        s.gagg[rows] = dot_nt(zz, nf[D:]).astype(BF16)

    own, coarse = slice(0, N), slice(N, N + C)

    def fill_node(j, to):
        w = node_refs.w
        w[j, :256] = dot_tn(node_in[:N, pl.ds(aligned(to * 256, 128), 256)], s.n_gbefore[:N]).astype(BF16)
        w[j, 256:] = dot_tn(s.n_hidden[:N, pl.ds(aligned(to * 128, 128), 128)], s.n_lin[:N]).astype(BF16)

    node_job = node_weights_sum(links, node_refs, RN, fill_node, s.n_grad)
    next(total)
    for copy in node_swap:
        copy.wait_recv()
    node_pass_forward(own)
    node_pass_backward(own)
    next(node_job)
    next(total)
    next(node_job)
    s.slope[...] = silu_slope(before[...])
    s.coarse_base[...] = dot(node_in[N:, :D], nf[:D])
    s.edge_in_t[...] = jnp.transpose(edge_in[...])
    s.hidden_t[...] = jnp.transpose(s.hidden[...])
    for _ in total:
        pass
    node_in[N:, D:] = s.coarse_total[...]
    node_pass_forward(coarse)
    node_pass_backward(coarse)

    s.gnext[...] = s.v_edge_cot[...].astype(F32) + dot(s.recv_hot[...], s.gagg[...])
    alive = lax.broadcasted_iota(jnp.int32, (E, 1), 0) < live
    upstream = jnp.where(alive, s.gnext[...], 0.0)
    q = norm_backward(upstream, s.v_edge_gain[...], s.normed[...], s.inverse[...])
    s.lin[...] = q
    s.gbefore[...] = (dot_nt(q, es[...]) * s.slope[...]).astype(BF16)
    gbefore = s.gbefore


    def fill_ea(j, to):
        ea_refs.w[j] = dot(s.edge_in_t[pl.ds(aligned(to * 384, 128), 256), :], gbefore[...]).astype(BF16)

    def fill_eb(j, to):
        first = dot(s.edge_in_t[pl.ds(aligned(to * 384 + 256, 128), 128), :], gbefore[...])
        second = dot(s.hidden_t[pl.ds(aligned(to * 128, 128), 128), :], s.lin[...])
        eb_refs.w[j, :128] = first.astype(BF16)
        eb_refs.w[j, 128:] = second.astype(BF16)

    ea_job = edge_weights_sum(links, ea_refs, RE, fill_ea, s.ea_grad)
    eb_job = edge_weights_sum(links, eb_refs, RE, fill_eb, s.eb_grad)
    next(ea_job)
    next(node_job)
    next(eb_job)
    moved = s.moved
    moved[...] = dot_nt(gbefore[...], ef[D : 2 * D]).astype(BF16)
    back_out, back_in = s.back_out, s.back_in
    back_out[...] = to_slots(dot(s.send_hot_t[512:1024], moved[...]))
    back_wait = links.send_many(
        G, graph_peer, lambda m: back_out.at[m], back_in.at[g], back_in.at[pl.ds(0, G - 1)]
    )
    back_in[g] = back_out[g]
    next(ea_job)
    next(eb_job)
    s.part_grads[...] = dot(s.send_hot_t[:512], moved[...])
    s.coarse_part[...] = dot(s.send_hot_t[1024:], moved[...])
    moved[...] = dot_nt(gbefore[...], ef[2 * D :]).astype(BF16)
    s.coarse_part[...] = s.coarse_part[...] + dot(s.recv_hot_t[N:], moved[...])
    coarse_grad = s.coarse_grad
    total = coarse_sum_by_chip(links, s, coarse_grad)
    next(total)
    s.recv_own[...] = dot(s.recv_hot_t[:N], moved[...])
    s.edge_grad[...] = s.gnext[...] + dot_nt(gbefore[...], ef[:D])
    s.direct[:N] = s.v_node_cot[...].astype(F32) + dot_nt(s.n_gbefore[:N], nf[:D])
    s.direct[N:] = s.v_coarse_cot[...].astype(F32) + dot_nt(s.n_gbefore[N:], nf[:D])
    extra = node_refs.extra
    first = dot_tn(node_in[N:, pl.ds(aligned(y * 256, 128), 256)], s.n_gbefore[N:])
    extra[0, :RN] = first[:RN]
    extra[1, : 256 - RN] = first[RN:]
    extra[1, 256 - RN : RN] = dot_tn(s.n_hidden[N:, pl.ds(aligned(y * 128, 128), 128)], s.n_lin[N:])
    extra[:, RN:] = jnp.zeros((NC, NZ * ZR - RN, D), F32)
    next(node_job)
    next(ea_job)
    next(eb_job)
    next(total)
    next(ea_job)
    next(node_job)
    next(eb_job)
    next(ea_job)

    back_wait()
    s.halo[...] = from_slots(back_in[...])
    s.part_grads[...] = s.part_grads[...] + dot(s.halo_hot_t[...], s.halo[...])
    p_y = s.p_y
    for j in range(4):
        p_y[j] = s.part_grads[pl.ds(aligned(xor4(y, j) * N, 16), N), :].astype(BF16)
    node_grad = s.node_grad
    part_job = halving(
        links, p_y, N // 2, s.p_a1, s.p_b1, s.p_a2, s.p_b2, lambda j: links.at(y=xor4(y, j)), node_grad
    )
    next(part_job)
    next(node_job)
    next(total)
    next(eb_job)
    next(ea_job)
    next(part_job)
    next(total)
    next(node_job)
    next(eb_job)
    for _ in part_job:
        pass
    node_grad[...] = node_grad[...] + s.direct[:N] + s.recv_own[...]
    next(ea_job)
    next(total)
    next(node_job)
    next(eb_job)
    for _ in total:
        pass
    coarse_grad[...] = coarse_grad[...] + s.direct[N:]
    for job in (ea_job, node_job, eb_job):
        for _ in job:
            pass
    links.finish()


def finish(*refs):
    sources, results, held, sems = refs[:6], refs[6:13], refs[13:17], refs[17]
    ea_grad, eb_grad, n_grad = sources[3:]
    ef, es, nf, ns = held
    stores = [
        pltpu.make_async_copy(src, dst, sems.at[k])
        for k, (src, dst) in enumerate(zip((*sources[:3], *held), results))
    ]
    for k in range(3):
        stores[k].start()
    for i in range(4 * RE // 16):
        row = i * 16
        pieces, core, block = (ea_grad, eb_grad)[i // 16], (i // 8) % 2, i % 8
        out, at = (ef, row) if row < 384 else (es, row - 384)
        for j in range(NX):
            out[at : at + 16, j * 128 : (j + 1) * 128] = pieces[core, j * NZ + block].astype(F32)
    stores[3].start()
    stores[4].start()
    for i in range(2 * RN // ZR):
        row = i * ZR
        out, at = (nf, row) if row < 256 else (ns, row - 256)
        for j in range(NX):
            out[at : at + ZR, j * 128 : (j + 1) * 128] = n_grad[row // RN, j, (row % RN) // ZR].astype(F32)
    stores[5].start()
    stores[6].start()
    for copy in stores:
        copy.wait()


def program(
    node_lat, coarse_lat, edge_lat, senders, receivers, halo_rows, edge_live, edge_first, edge_second,
    node_first, node_second, edge_gain, node_gain, node_cotangent, coarse_cotangent, edge_cotangent,
):
    vmem, anywhere = pl.BlockSpec(memory_space=pltpu.VMEM), pl.BlockSpec(memory_space=pl.ANY)
    semaphores = [pltpu.SemaphoreType.DMA((count,)) for count in (SENDS, SENDS, LOCALS)]
    results = pl.pallas_call(
        body,
        out_shape=[pltpu.VMEM(*v) for v in OUTPUTS.values()],
        in_specs=[anywhere] * len(INPUTS),
        out_specs=[vmem] * len(OUTPUTS),
        scratch_shapes=[pltpu.VMEM(*v) for d in (SCRATCH, EDGE_JOB, EDGE_JOB, NODE_JOB) for v in d.values()]
        + [pltpu.SMEM((1,), jnp.int32)] + semaphores,
        compiler_params=pltpu.CompilerParams(
            collective_id=0, has_side_effects=True, vmem_limit_bytes=60 * 1024 * 1024
        ),
        name="layer",
    )(
        node_lat,
        coarse_lat,
        edge_lat,
        senders.reshape(1, E),
        receivers.reshape(1, E),
        halo_rows.T,
        edge_live,
        edge_first,
        edge_second,
        node_first,
        node_second,
        edge_gain.reshape(1, D),
        node_gain.reshape(1, D),
        node_cotangent,
        coarse_cotangent,
        edge_cotangent,
    )
    shapes = [(N, D), (C, D), (E, D), (384, D), (128, D), (256, D), (128, D)]
    return pl.pallas_call(
        finish,
        out_shape=[jax.ShapeDtypeStruct(v, F32) for v in shapes],
        in_specs=[vmem] * 6,
        out_specs=[anywhere] * 7,
        scratch_shapes=[pltpu.VMEM(v, F32) for v in shapes[3:]] + [pltpu.SemaphoreType.DMA((7,))],
        compiler_params=pltpu.CompilerParams(vmem_limit_bytes=60 * 1024 * 1024),
        name="finish",
    )(*(pltpu.with_memory_space_constraint(v, pltpu.VMEM) for v in results))


def solution(mesh):
    rows = P(("graph", "feat"), None)
    return jax.shard_map(
        program,
        mesh=mesh,
        in_specs=(
            rows, P(), rows, P(("graph", "feat")), P(("graph", "feat")), rows, P(("graph", "feat")),
            P("feat", None), P("feat", None), P("feat", None), P("feat", None), P(), P(), rows, P(), rows,
        ),
        out_specs=(
            rows, P(), rows, P("feat", None), P("feat", None), P("feat", None), P("feat", None),
        ),
        check_vma=False,
    )
```
